256 devices in a mesh: row: 32 (over x, z_hi, core), col: 8 (over y, z_lo).
Axes of the slice: x: 4, y: 4, z: 8 (z_hi: 4, z_lo: 2; z = z_hi * 2 + z_lo), core: 2. Of those that a mesh axis runs over, the one named last changes fastest.
Arguments:
- object_slab: float32 [2, 8192, 2048], P(None, 'row', 'col'), may hold values from -6 to 6
- probe_modes: float32 [2, 2, 128, 128], replicated, may hold values from -6 to 6
- intensities: float32 [32, 8, 24, 128, 128], P('row', 'col'), may hold values from 0 to 16
- positions: int32 [32, 8, 24, 2], P('row', 'col'), may hold values from -64 to 8127, as said below
- live_counts: int32 [32, 8], replicated, may hold values from 1 to 24, as said below
Outputs:
- object_final: float32 [2, 8192, 2048], P(None, 'row', 'col')
- probe_final: float32 [2, 2, 128, 128], replicated
The draws below stay inside these ranges and needn't reach their ends.
Inputs may be any that keep to these rules, and one draw needn't show every extreme that they name: Device (r, c) has live frames in slots 0 to live_counts[r, c] - 1; at least one device has 24. `positions`: Top-left pixel (row, column) of each slot's frame. The frame's centre (row + 64, column + 64) lies in the tile of the device that holds the slot: r * 256 <= row + 64 < (r + 1) * 256 and c * 256 <= column + 64 < (c + 1) * 256, for slots that are not live too.
All inputs are finite; a program needn't handle non-finite values.
Results may differ from the reference program's by a relative error of at most 0.0003.
Values sent between devices are 32-bit elements; how exact they have to be, the bound alone decides.
A program may use at most 128 MiB of HBM per device.

```python
import jax
import jax.numpy as jnp
from jax import lax

W = 128
MODES = 2
TR = 256
TC = 256
CAP = 24
ITERS = 2
NR = 8192
NC = 2048
N_ROW = 32
N_COL = 8


def draw_live_counts(key, part):
    key = jax.random.fold_in(key, 11)
    key_left, key_right, key_pick = jax.random.split(key, 3)
    grid_rows = NR // TR
    grid_cols = NC // TC
    factor_left = jax.random.randint(key_left, (grid_rows, grid_cols), 0, CAP)
    factor_right = jax.random.randint(key_right, (grid_rows, grid_cols), 0, CAP)
    frame_loads = 1 + factor_left * factor_right // CAP
    chosen_one = jax.random.randint(key_pick, (), 0, grid_rows * grid_cols)
    frame_loads = frame_loads.reshape(-1).at[chosen_one].set(CAP)
    return frame_loads.reshape(grid_rows, grid_cols).astype(jnp.int32)


def draw_positions(key, part):
    key = jax.random.fold_in(key, 23)
    key_rows, key_cols = jax.random.split(key)
    grid_rows = NR // TR
    grid_cols = NC // TC
    centre_rows = jax.random.randint(key_rows, (grid_rows, grid_cols, CAP), 0, TR)
    centre_cols = jax.random.randint(key_cols, (grid_rows, grid_cols, CAP), 0, TC)
    tile_rows = (jnp.arange(grid_rows, dtype=jnp.int32) * TR)[:, None, None]
    tile_cols = (jnp.arange(grid_cols, dtype=jnp.int32) * TC)[None, :, None]
    corner_rows = centre_rows + tile_rows - W // 2
    corner_cols = centre_cols + tile_cols - W // 2
    return jnp.stack([corner_rows, corner_cols], axis=-1).astype(jnp.int32)


def block_levels(stream_key, extent, cuts, smallest, high):
    gain = 1.0
    for axis_at, parts in cuts:
        heights = jax.random.uniform(jax.random.fold_in(jax.random.fold_in(stream_key, 6), axis_at), (parts,), jnp.float32, smallest / len(cuts), high / len(cuts))
        gain = gain * jnp.repeat(jnp.exp(heights), extent[axis_at] // parts).reshape((-1,) + (1,) * (len(extent) - 1 - axis_at))
    return gain


def normal_values(key, extent, deviation, reach, cuts=(), kind=jnp.bfloat16):
    loudness = block_levels(key, extent, cuts, -0.22, 0.18) if cuts else 1.0
    values = jax.random.normal(key, extent, jnp.float32) * deviation * loudness
    return jnp.minimum(jnp.maximum(values, -reach), reach).astype(kind)


def setup_inputs(seed: int = 0) -> dict:
    splits = jax.random.split(jax.random.key(seed), 6)
    return {
        "object_slab": normal_values(splits[0], (2, NR, NC), 1.0, 6.0, ((1, 32), (2, 8)), jnp.float32),
        "probe_modes": normal_values(splits[1], (MODES, 2, W, W), 1.0, 6.0, (), jnp.float32),
        "intensities": jnp.clip(16.0 * jax.random.uniform(splits[2], (N_ROW, N_COL, CAP, W, W), jnp.float32) ** block_levels(splits[2], (N_ROW, N_COL, CAP, W, W), ((0, 32), (1, 8)), -0.2, 0.2), 0.0, 16.0),
        "positions": draw_positions(jax.random.fold_in(splits[5], 71), 0),
        "live_counts": draw_live_counts(jax.random.fold_in(splits[5], 71), 0),
    }


AMP_FLOOR = 0.25
OBJECT_REG = 1.0
PROBE_REG = 1.0

def frame_terms(padded, probe_now, amplitude, corner, live_flag):
    margin = W // 2
    row_at = corner[0].astype(jnp.int32) + margin
    col_at = corner[1].astype(jnp.int32) + margin
    obj_patch = lax.dynamic_slice(padded, (jnp.int32(0), row_at, col_at), (2, W, W))
    object_c = obj_patch[0] + 1j * obj_patch[1]
    probe_c = probe_now[:, 0] + 1j * probe_now[:, 1]
    far_field = jnp.fft.fft2(probe_c * object_c[None], norm='ortho')
    model_sum = lax.optimization_barrier(jnp.sum(jnp.real(far_field) ** 2 + jnp.imag(far_field) ** 2, axis=0))
    amp_ratio = amplitude / jnp.maximum(jnp.sqrt(model_sum), AMP_FLOOR)
    scaled = far_field * ((1.0 - amp_ratio) * live_flag)[None]
    residual = jnp.fft.ifft2(scaled, norm='ortho')
    object_term = lax.optimization_barrier(jnp.sum(jnp.conj(probe_c) * residual, axis=0))
    probe_term = jnp.conj(object_c)[None] * residual
    lighting = live_flag * lax.optimization_barrier(jnp.sum(probe_now * probe_now, axis=(0, 1)))
    grad_piece = jnp.stack([jnp.real(object_term), jnp.imag(object_term), lighting])
    probe_piece = jnp.stack([jnp.real(probe_term), jnp.imag(probe_term)], axis=1)
    obj_power = live_flag * (obj_patch[0] ** 2 + obj_patch[1] ** 2)
    return (grad_piece, probe_piece, obj_power, row_at, col_at)

def reference(object_slab, probe_modes, intensities, positions, live_counts):
    margin = W // 2
    slot_total = N_ROW * N_COL * CAP
    amplitudes = jnp.sqrt(intensities).reshape(slot_total, W, W)
    corners = positions.reshape(slot_total, 2)
    slot_ids = jnp.arange(CAP, dtype=jnp.int32)
    live = (slot_ids[None, None, :] < live_counts[:, :, None]).astype(jnp.float32).reshape(slot_total)
    current = object_slab
    probe_now = probe_modes
    for sweep_id in range(ITERS):
        padded = jnp.pad(current, ((0, 0), (margin, margin), (margin, margin)))

        def visit(carried, scan_item):
            grad_sum, probe_sum, power_sum = carried
            amplitude, corner, live_flag = scan_item
            grad_piece, probe_piece, obj_power, row_at, col_at = frame_terms(padded, probe_now, amplitude, corner, live_flag)
            anchor = (jnp.int32(0), row_at, col_at)
            before = lax.dynamic_slice(grad_sum, anchor, (3, W, W))
            grad_sum = lax.dynamic_update_slice(grad_sum, before + grad_piece, anchor)
            return ((grad_sum, probe_sum + probe_piece, power_sum + obj_power), live_flag)
        initial = (jnp.zeros((3, NR + 2 * margin, NC + 2 * margin), jnp.float32), jnp.zeros((MODES, 2, W, W), jnp.float32), jnp.zeros((W, W), jnp.float32))
        totals, unused = lax.scan(visit, initial, (amplitudes, corners, live))
        grad_sum, probe_sum, power_sum = totals
        interior = grad_sum[:, margin:margin + NR, margin:margin + NC]
        current = current - interior[:2] / (interior[2] + OBJECT_REG)
        probe_now = probe_now - probe_sum / (power_sum + PROBE_REG)
    return (current, probe_now)
```

```python
import functools

import jax
import jax.numpy as jnp
import ml_dtypes
import numpy as np
from jax import lax
from jax.experimental import pallas as pl
from jax.experimental.pallas import tpu as pltpu
from jax.sharding import PartitionSpec as P

ITERS = 2
W = 128
MARGIN = 64
TILE = 256
EXT = TILE + 2 * MARGIN
SLOTS = 24
BATCH = 2
OBJECT_REG = 1.0
PROBE_REG = 1.0
FLOOR_SQ = 0.0625
TINY = 1e-36
N_ROW = 32
N_COL = 8
N_PLANE = 16
N_Z = 8
VMEM_LIMIT = 60 * 1024 * 1024
MESH = pl.DeviceIdType.MESH


def dft_parts():
    counter = np.arange(W)
    angles = (counter[:, None] * counter[None, :] % W) * (2.0 * np.pi / W)
    cosine = np.cos(angles) / np.sqrt(W)
    sine = np.sin(angles) / np.sqrt(W)
    fore = np.block([[cosine, sine], [-sine, cosine]])
    back = np.block([[cosine, -sine], [sine, cosine]])

    def split(table):
        high = table.astype(np.float32).astype(ml_dtypes.bfloat16)
        low = (table - high.astype(np.float64)).astype(np.float32).astype(ml_dtypes.bfloat16)
        return high, low

    fore_hi, fore_lo = split(fore)
    back_hi, back_lo = split(back)
    right_first = np.concatenate([back_hi, back_hi, back_lo], axis=0)
    left_first = np.concatenate([fore_hi, fore_lo, fore_hi], axis=1)
    left_second = np.concatenate([back_hi, back_lo, back_hi], axis=1)
    right_second = np.concatenate([fore_hi, fore_hi, fore_lo], axis=0)
    return right_first, left_first, left_second, right_second


def split_two(value):
    high = value.astype(jnp.bfloat16)
    low = (value - high.astype(jnp.float32)).astype(jnp.bfloat16)
    return high, low


def dot(left, right):
    return jnp.dot(left, right, preferred_element_type=jnp.float32)


def frames_kernel(
    spots, count, obj, probe, intens, right_first, left_first, left_second, right_second,
    grad, sums,
):
    grad[...] = jnp.zeros_like(grad)
    sums[...] = jnp.zeros_like(sums)
    own = count[0]
    lane = lax.broadcasted_iota(jnp.int32, (W, W), 1)
    lighting = sum(probe[m, k] * probe[m, k] for m in range(2) for k in range(2))

    def batch(turn, carry):
        patches, places, flags, rows = [], [], [], []
        for member in range(BATCH):
            slot = turn * BATCH + member
            row = spots[slot, 0]
            col = spots[slot, 1]
            first = lax.shift_right_logical(col, 7)
            shift = lax.bitwise_and(col, 127)
            second = jnp.where(first == 2, 0, first + 1)
            back = lax.bitwise_and(128 - shift, 127)
            keep = lane >= shift
            patch = []
            for k in range(2):
                one = obj[k, first, pl.ds(row, W), :]
                two = obj[k, second, pl.ds(row, W), :]
                patch.append(pltpu.roll(jnp.where(keep, one, two), back, 1))
            patches.append(patch)
            places.append((row, first, second, shift, keep))
            flags.append(jnp.where(slot < own, 1.0, 0.0).astype(jnp.float32))
            for m in range(2):
                real = probe[m, 0] * patch[0] - probe[m, 1] * patch[1]
                imag = probe[m, 0] * patch[1] + probe[m, 1] * patch[0]
                real_hi, real_lo = split_two(real)
                imag_hi, imag_lo = split_two(imag)
                rows.append(
                    jnp.concatenate([real_hi, imag_hi, real_lo, imag_lo, real_hi, imag_hi], axis=1)
                )
        mid = dot(jnp.concatenate(rows, axis=0), right_first[...])
        rows = []
        for member in range(BATCH):
            base = member * 2 * W
            real_hi, real_lo = split_two(
                jnp.concatenate([mid[base : base + W, :W], mid[base + W : base + 2 * W, :W]], axis=1)
            )
            imag_hi, imag_lo = split_two(
                jnp.concatenate([mid[base : base + W, W:], mid[base + W : base + 2 * W, W:]], axis=1)
            )
            stacked = jnp.concatenate([real_hi, imag_hi, real_hi, imag_hi, real_lo, imag_lo], axis=0)
            far = dot(left_first[...], stacked)
            far_real = far[:W]
            far_imag = far[W:]
            power = far_real * far_real + far_imag * far_imag
            model = jnp.maximum(power[:, :W] + power[:, W:], FLOOR_SQ)
            frame = intens[turn * BATCH + member]
            ratio = frame * lax.rsqrt(jnp.maximum(frame * model, TINY))
            factor = (1.0 - ratio) * flags[member]
            factor = jnp.concatenate([factor, factor], axis=1)
            real_hi, real_lo = split_two(far_real * factor)
            imag_hi, imag_lo = split_two(far_imag * factor)
            stacked = jnp.concatenate([real_hi, imag_hi, real_hi, imag_hi, real_lo, imag_lo], axis=0)
            near = dot(left_second[...], stacked)
            real_hi, real_lo = split_two(near[:W])
            imag_hi, imag_lo = split_two(near[W:])
            for m in range(2):
                cut = slice(m * W, (m + 1) * W)
                rows.append(
                    jnp.concatenate(
                        [real_hi[:, cut], imag_hi[:, cut], real_lo[:, cut], imag_lo[:, cut],
                         real_hi[:, cut], imag_hi[:, cut]], axis=1,
                    )
                )
        resid = dot(jnp.concatenate(rows, axis=0), right_second[...])
        terms = [None] * 5
        for member in range(BATCH):
            row, first, second, shift, keep = places[member]
            obj_real, obj_imag = patches[member]
            grad_real = 0.0
            grad_imag = 0.0
            adds = []
            for m in range(2):
                base = (member * 2 + m) * W
                real = resid[base : base + W, :W]
                imag = resid[base : base + W, W:]
                grad_real = grad_real + probe[m, 0] * real + probe[m, 1] * imag
                grad_imag = grad_imag + probe[m, 0] * imag - probe[m, 1] * real
                adds.append(obj_real * real + obj_imag * imag)
                adds.append(obj_real * imag - obj_imag * real)
            adds.append((obj_real * obj_real + obj_imag * obj_imag) * flags[member])
            for k in range(5):
                terms[k] = adds[k] if member == 0 else terms[k] + adds[k]
            for k, piece in enumerate((grad_real, grad_imag, lighting * flags[member])):
                turned = pltpu.roll(piece, shift, 1)
                grad[k, first, pl.ds(row, W), :] += jnp.where(keep, turned, 0.0)
                grad[k, second, pl.ds(row, W), :] += jnp.where(keep, 0.0, turned)
        for k in range(5):
            sums[k] += terms[k]
        return carry

    lax.fori_loop(0, (own + BATCH - 1) // BATCH, batch, 0)


def frames(spots, count, obj, probe, intens, tables):
    vmem = pl.BlockSpec(memory_space=pltpu.VMEM)
    smem = pl.BlockSpec(memory_space=pltpu.SMEM)
    return pl.pallas_call(
        frames_kernel,
        out_shape=(
            jax.ShapeDtypeStruct((3, 3, EXT, W), jnp.float32),
            jax.ShapeDtypeStruct((5, W, W), jnp.float32),
        ),
        in_specs=[smem, smem] + [vmem] * 7,
        out_specs=(vmem, vmem),
        compiler_params=pltpu.CompilerParams(vmem_limit_bytes=VMEM_LIMIT),
        name="frames",
    )(spots, count, obj, probe, intens, *tables)


def places():
    row = lax.axis_index("row")
    col = lax.axis_index("col")
    core = row % 2
    z_hi = (row // 2) % 4
    x = row // 8
    y = col // 2
    z_lo = col % 2
    return row, col, core, x, y, z_hi, z_lo


def spread_kernel(fold, halo, *refs):
    refs = list(refs)
    take = lambda n: [refs.pop(0) for _ in range(n)]
    if fold:
        obj_in, probe_in, grad, sums = take(4)
        obj_out, probe_out = take(2)
        (pair_buf, rs_src, rs_buf, z_src, z_buf, ag_buf, ag_pair, fold_r, fold_mid, fold_cs, fold_c) = take(11)
        (pair_ss, pair_rs, rs_ss, rs_rs, z_ss, z_rs, ag_ss, ag_rs, agp_ss, agp_rs, fr_ss, fr_rs, fc_ss, fc_rs) = take(14)
    else:
        (obj_in,) = take(1)
        (obj_out,) = take(1)
    if halo:
        halo_cs, halo_c, halo_r, hc_ss, hc_rs, hr_ss, hr_rs = take(7)

    row, col, core, x, y, z_hi, z_lo = places()
    plane = x * 4 + y
    z = z_hi * 2 + z_lo
    up = (lax.rem(row + N_ROW - 1, N_ROW), col)
    down = (lax.rem(row + 1, N_ROW), col)
    left = (row, lax.rem(col + N_COL - 1, N_COL))
    right = (row, lax.rem(col + 1, N_COL))
    pair = (row + 1 - 2 * core, col)
    has_up = row > 0
    has_down = row < N_ROW - 1
    has_left = col > 0
    has_right = col < N_COL - 1

    def plane_mate(step):
        other = lax.rem(plane + step, N_PLANE)
        return other, (((other // 4) * 4 + z_hi) * 2 + core, (other % 4) * 2 + z_lo)

    def z_mate(step):
        other = lax.rem(z + step, N_Z)
        return other, ((x * 4 + other // 2) * 2 + core, y * 2 + other % 2)

    def copy(src, dst, ss, rs, device):
        return pltpu.make_async_remote_copy(
            src_ref=src, dst_ref=dst, send_sem=ss, recv_sem=rs, device_id=device, device_id_type=MESH
        )

    barrier = pltpu.get_barrier_semaphore()

    def greet(device):
        pl.semaphore_signal(barrier, inc=1, device_id=device, device_id_type=MESH)

    for device in (up, down, left, right):
        greet(device)
    greeted = 4
    if fold:
        greet(pair)
        lax.fori_loop(1, N_PLANE, lambda s, c: (greet(plane_mate(s)[1]), c)[1], 0)
        lax.fori_loop(1, N_Z, lambda s, c: (greet(z_mate(s)[1]), c)[1], 0)
        greeted += 1 + N_PLANE - 1 + N_Z - 1
    pl.semaphore_wait(barrier, greeted)

    lane = lax.broadcasted_iota(jnp.int32, (W, W), 1)
    low = lane < MARGIN

    def half(value):
        return pltpu.roll(value, MARGIN, 1)

    def rs_copy(step):
        other, device = plane_mate(step)
        return copy(rs_src.at[other], rs_buf.at[plane], rs_ss.at[step], rs_rs.at[step], device)

    def rs_arrival(step):
        other = lax.rem(plane + N_PLANE - step, N_PLANE)
        return copy(rs_src.at[other], rs_buf.at[other], rs_ss.at[step], rs_rs.at[step], up)

    def z_copy(step):
        return copy(z_src, z_buf.at[z], z_ss.at[step], z_rs.at[step], z_mate(step)[1])

    def z_arrival(step):
        other = lax.rem(z + N_Z - step, N_Z)
        return copy(z_src, z_buf.at[other], z_ss.at[step], z_rs.at[step], up)

    def ag_copy(step):
        return copy(ag_buf.at[plane], ag_buf.at[plane], ag_ss.at[step], ag_rs.at[step], plane_mate(step)[1])

    def ag_arrival(step):
        other = lax.rem(plane + N_PLANE - step, N_PLANE)
        return copy(ag_buf.at[other], ag_buf.at[other], ag_ss.at[step], ag_rs.at[step], up)

    def each(count, act):
        lax.fori_loop(1, count, lambda s, c: (act(s), c)[1], 0)

    if fold:
        pair_copies = [
            copy(sums.at[pl.ds(2 * (1 - core), 2)], pair_buf.at[pl.ds(0, 2)], pair_ss.at[0], pair_rs.at[0], pair),
            copy(sums.at[pl.ds(4, 1)], pair_buf.at[pl.ds(2, 1)], pair_ss.at[1], pair_rs.at[1], pair),
        ]
        fr_copies = [
            copy(grad.at[:, :, pl.ds(0, MARGIN)], fold_r.at[0], fr_ss.at[0], fr_rs.at[0], up),
            copy(grad.at[:, :, pl.ds(TILE + MARGIN, MARGIN)], fold_r.at[1], fr_ss.at[1], fr_rs.at[1], down),
        ]
        for one in pair_copies + fr_copies:
            one.start()
        for one in pair_copies:
            one.wait_recv()
        for k in range(3):
            own = sums[4] if k == 2 else sums[2 * core + k]
            rs_src[:, k] = own + pair_buf[k]
        each(N_PLANE, lambda s: rs_copy(s).start())
        rs_buf[plane] = rs_src[plane]

        for one in fr_copies:
            one.wait_recv()
        fold_mid[...] = grad[:, :, MARGIN : MARGIN + TILE, :]
        fold_mid[:, :, TILE - MARGIN :, :] += jnp.where(has_down, fold_r[0], 0.0)
        fold_mid[:, :, :MARGIN, :] += jnp.where(has_up, fold_r[1], 0.0)
        for k in range(3):
            top = fold_mid[k, 2, :W, :]
            low_part = fold_mid[k, 2, W:, :]
            fold_cs[0, k] = jnp.where(low, half(top), low_part)
            fold_cs[1, k] = jnp.where(low, top, half(low_part))
        fc_copies = [
            copy(fold_cs.at[0], fold_c.at[0], fc_ss.at[0], fc_rs.at[0], left),
            copy(fold_cs.at[1], fold_c.at[1], fc_ss.at[1], fc_rs.at[1], right),
        ]
        for one in fc_copies:
            one.start()

        each(N_PLANE, lambda s: rs_arrival(s).wait_recv())
        total = rs_buf[0]
        for other in range(1, N_PLANE):
            total = total + rs_buf[other]
        z_src[...] = total
        z_buf[z] = total
        each(N_Z, lambda s: z_copy(s).start())

        for one in fc_copies:
            one.wait_recv()
        new_parts = {}
        sums_of = {}
        for k in range(3):
            from_right = jnp.where(has_right, fold_c[0, k], 0.0)
            from_left = jnp.where(has_left, fold_c[1, k], 0.0)
            sums_of[k, 0, 0] = fold_mid[k, 0, :W, :] + jnp.where(low, from_left, 0.0)
            sums_of[k, 0, 1] = fold_mid[k, 0, W:, :] + jnp.where(low, half(from_left), 0.0)
            sums_of[k, 1, 0] = fold_mid[k, 1, :W, :] + jnp.where(low, 0.0, half(from_right))
            sums_of[k, 1, 1] = fold_mid[k, 1, W:, :] + jnp.where(low, 0.0, from_right)
        for part in range(2):
            for block in range(2):
                weight = 1.0 / (sums_of[2, part, block] + OBJECT_REG)
                for k in range(2):
                    start = MARGIN + block * W
                    new = obj_in[k, part, start : start + W, :] - sums_of[k, part, block] * weight
                    if halo:
                        obj_out[k, part, start : start + W, :] = new
                    else:
                        obj_out[k, block * W : (block + 1) * W, part * W : (part + 1) * W] = new
    else:
        for k in range(2):
            for part in range(2):
                obj_out[k, part, MARGIN : MARGIN + TILE, :] = obj_in[k, :, part * W : (part + 1) * W]

    if halo:
        for k in range(2):
            top = obj_out[k, 0, MARGIN : MARGIN + W, :]
            low_part = obj_out[k, 0, MARGIN + W : MARGIN + TILE, :]
            halo_cs[0, k] = jnp.where(low, top, half(low_part))
            top = obj_out[k, 1, MARGIN : MARGIN + W, :]
            low_part = obj_out[k, 1, MARGIN + W : MARGIN + TILE, :]
            halo_cs[1, k] = jnp.where(low, half(top), low_part)
        hc_copies = [
            copy(halo_cs.at[0], halo_c.at[0], hc_ss.at[0], hc_rs.at[0], left),
            copy(halo_cs.at[1], halo_c.at[1], hc_ss.at[1], hc_rs.at[1], right),
        ]
        for one in hc_copies:
            one.start()

    if fold:
        each(N_Z, lambda s: z_arrival(s).wait_recv())
        total = z_buf[0]
        for other in range(1, N_Z):
            total = total + z_buf[other]
        weight = 1.0 / (total[2] + PROBE_REG)
        for k in range(2):
            ag_buf[plane, k] = probe_in[core, k, plane] - total[k] * weight
        each(N_PLANE, lambda s: ag_copy(s).start())

    if halo:
        for one in hc_copies:
            one.wait_recv()
        for k in range(2):
            from_right = jnp.where(has_right, halo_c[0, k], 0.0)
            from_left = jnp.where(has_left, halo_c[1, k], 0.0)
            obj_out[k, 2, MARGIN : MARGIN + W, :] = jnp.where(low, from_right, half(from_left))
            obj_out[k, 2, MARGIN + W : MARGIN + TILE, :] = jnp.where(low, half(from_right), from_left)
        hr_copies = [
            copy(obj_out.at[:, :, pl.ds(MARGIN, MARGIN)], halo_r.at[0], hr_ss.at[0], hr_rs.at[0], up),
            copy(obj_out.at[:, :, pl.ds(TILE, MARGIN)], halo_r.at[1], hr_ss.at[1], hr_rs.at[1], down),
        ]
        for one in hr_copies:
            one.start()

    if fold:
        each(N_PLANE, lambda s: ag_arrival(s).wait_recv())
        agp = copy(ag_buf, ag_pair, agp_ss.at[0], agp_rs.at[0], pair)
        agp.start()

    if halo:
        for one in hr_copies:
            one.wait_recv()
        obj_out[:, :, TILE + MARGIN :, :] = jnp.where(has_down, halo_r[0], 0.0)
        obj_out[:, :, :MARGIN, :] = jnp.where(has_up, halo_r[1], 0.0)

    if fold:
        for k in range(2):
            probe_out[core, k] = ag_buf[:, k]
        agp.wait_recv()
        for k in range(2):
            probe_out[1 - core, k] = ag_pair[:, k]
        for one in pair_copies + fr_copies + fc_copies:
            one.wait_send()
        each(N_PLANE, lambda s: rs_copy(s).wait_send())
        each(N_Z, lambda s: z_copy(s).wait_send())
        each(N_PLANE, lambda s: ag_copy(s).wait_send())
        agp.wait_send()
    if halo:
        for one in hc_copies + hr_copies:
            one.wait_send()


def spread(fold, halo, number, *operands):
    vmem = pl.BlockSpec(memory_space=pltpu.VMEM)
    dma = pltpu.SemaphoreType.DMA
    f32 = jnp.float32
    outs = []
    if halo:
        outs.append(jax.ShapeDtypeStruct((2, 3, EXT, W), f32))
    else:
        outs.append(jax.ShapeDtypeStruct((2, TILE, TILE), f32))
    scratch = []
    if fold:
        outs.append(jax.ShapeDtypeStruct((2, 2, 16, 8, W), f32))
        scratch += [
            pltpu.VMEM((3, 16, 8, W), f32),
            pltpu.VMEM((16, 3, 8, W), f32),
            pltpu.VMEM((16, 3, 8, W), f32),
            pltpu.VMEM((3, 8, W), f32),
            pltpu.VMEM((8, 3, 8, W), f32),
            pltpu.VMEM((16, 2, 8, W), f32),
            pltpu.VMEM((16, 2, 8, W), f32),
            pltpu.VMEM((2, 3, 3, MARGIN, W), f32),
            pltpu.VMEM((3, 3, TILE, W), f32),
            pltpu.VMEM((2, 3, W, W), f32),
            pltpu.VMEM((2, 3, W, W), f32),
            dma((2,)), dma((2,)), dma((16,)), dma((16,)), dma((8,)), dma((8,)), dma((16,)), dma((16,)),
            dma((1,)), dma((1,)), dma((2,)), dma((2,)), dma((2,)), dma((2,)),
        ]
    if halo:
        scratch += [
            pltpu.VMEM((2, 2, W, W), f32),
            pltpu.VMEM((2, 2, W, W), f32),
            pltpu.VMEM((2, 2, 3, MARGIN, W), f32),
            dma((2,)), dma((2,)), dma((2,)), dma((2,)),
        ]
    return pl.pallas_call(
        functools.partial(spread_kernel, fold, halo),
        out_shape=tuple(outs),
        in_specs=[vmem] * len(operands),
        out_specs=(vmem,) * len(outs),
        scratch_shapes=scratch,
        compiler_params=pltpu.CompilerParams(
            collective_id=number, has_side_effects=True, vmem_limit_bytes=VMEM_LIMIT
        ),
        name="spread" + str(number),
    )(*operands)


def per_device(object_slab, probe_modes, intensities, positions, live_counts):
    row_id = lax.axis_index("row")
    col_id = lax.axis_index("col")
    tables = [jnp.asarray(table) for table in dft_parts()]
    anchors = jnp.stack([row_id * TILE - MARGIN, col_id * TILE])
    spots = positions[0, 0] - anchors[None]
    spots = jnp.where(spots < 0, spots + EXT, spots).astype(jnp.int32)
    count = live_counts[row_id, col_id][None]
    intens = intensities[0, 0]
    probe = probe_modes
    (current,) = spread(False, True, 0, object_slab)
    for sweep in range(ITERS):
        grad, sums = frames(spots, count, current, probe, intens, tables)
        last = sweep == ITERS - 1
        current, probe = spread(
            True, not last, sweep + 1,
            current, probe.reshape(2, 2, 16, 8, W), grad, sums.reshape(5, 16, 8, W),
        )
        probe = probe.reshape(2, 2, W, W)
    return current, probe


def solution(mesh):
    return jax.shard_map(
        per_device,
        mesh=mesh,
        in_specs=(
            P(None, "row", "col"),
            P(),
            P("row", "col", None, None, None),
            P("row", "col", None, None),
            P(),
        ),
        out_specs=(P(None, "row", "col"), P()),
        check_vma=False,
    )
```

```python
import functools

import jax
import jax.numpy as jnp
import ml_dtypes
import numpy as np
from jax import lax
from jax.experimental import pallas as pl
from jax.experimental.pallas import tpu as pltpu
from jax.sharding import PartitionSpec as P

ITERS = 2
W = 128
MARGIN = 64
TILE = 256
EXT = TILE + 2 * MARGIN
SLOTS = 24
BATCH = 1
RING = 8
ORDER = 532164
OBJECT_REG = 1.0
PROBE_REG = 1.0
FLOOR_SQ = 0.0625
TINY = 1e-36
N_ROW = 32
N_COL = 8
N_PLANE = 16
N_Z = 8
FRAMES_VMEM = 20 * 1024 * 1024
SPREAD_VMEM = 16 * 1024 * 1024
MESH = pl.DeviceIdType.MESH


def dft_parts():
    counter = np.arange(W)
    angles = (counter[:, None] * counter[None, :] % W) * (2.0 * np.pi / W)
    cosine = np.cos(angles) / np.sqrt(W)
    sine = np.sin(angles) / np.sqrt(W)
    fore = np.block([[cosine, sine], [-sine, cosine]])
    back = np.block([[cosine, -sine], [sine, cosine]])

    def split(table):
        high = table.astype(np.float32).astype(ml_dtypes.bfloat16)
        low = (table - high.astype(np.float64)).astype(np.float32).astype(ml_dtypes.bfloat16)
        return high, low

    fore_hi, fore_lo = split(fore)
    back_hi, back_lo = split(back)
    return np.stack([fore_hi, fore_lo, back_hi, back_lo])


def split_two(value):
    high = value.astype(jnp.bfloat16)
    low = (value - high.astype(jnp.float32)).astype(jnp.bfloat16)
    return high, low


def dot(left, right):
    return jnp.dot(left, right, preferred_element_type=jnp.float32)


def frames_kernel(
    places, obj, probe, intens, tables,
    grad, sums, patch_buf, mid_buf, far_buf, back_buf, near_buf, light_buf,
):
    grad[...] = jnp.zeros_like(grad)
    sums[...] = jnp.zeros_like(sums)
    for buffer in (patch_buf, mid_buf, far_buf, back_buf, near_buf):
        buffer[...] = jnp.zeros_like(buffer)
    lighting = probe[0, 0] * probe[0, 0] + probe[0, 1] * probe[0, 1]
    light_buf[...] = lighting + probe[1, 0] * probe[1, 0] + probe[1, 1] * probe[1, 1]
    row_id = lax.axis_index("row")
    col_id = lax.axis_index("col")
    own = places[2 * SLOTS + row_id * N_COL + col_id]

    def on_left(high):
        return jnp.concatenate([tables[high], tables[high + 1], tables[high]], axis=1)

    def on_right(high):
        return jnp.concatenate([tables[high], tables[high], tables[high + 1]], axis=0)

    lane = lax.broadcasted_iota(jnp.int32, (W, W), 1)

    def place(slot):
        row = places[2 * slot] - (row_id * TILE - MARGIN)
        col = places[2 * slot + 1] - col_id * TILE
        col = jnp.where(col < 0, col + EXT, col)
        first = lax.shift_right_logical(col, 7)
        shift = lax.bitwise_and(col, 127)
        second = jnp.where(first == 2, 0, first + 1)
        return row, first, second, shift

    def member_slot(turn, member):
        slot = turn * BATCH + member
        flag = jnp.where(jnp.logical_and(slot >= 0, slot < own), 1.0, 0.0).astype(jnp.float32)
        return jnp.clip(slot, 0, SLOTS - 1), flag

    def last_product(turn):
        halves = []
        for member in range(BATCH):
            for m in range(2):
                halves.append(jnp.concatenate([near_buf[member, m], near_buf[member, m, :, : 2 * W]], axis=1))
        return dot(jnp.concatenate(halves, axis=0), on_right(0))

    def last_adds(turn, resid):
        ring = lax.bitwise_and(turn, RING - 1)
        terms = [None] * 5
        for member in range(BATCH):
            slot, flag = member_slot(turn, member)
            row, first, second, shift = place(slot)
            keep = lane >= shift
            obj_real = patch_buf[ring, member, 0]
            obj_imag = patch_buf[ring, member, 1]
            grad_real = 0.0
            grad_imag = 0.0
            adds = []
            for m in range(2):
                base = (member * 2 + m) * W
                real = resid[base : base + W, :W]
                imag = resid[base : base + W, W:]
                grad_real = grad_real + probe[m, 0] * real + probe[m, 1] * imag
                grad_imag = grad_imag + probe[m, 0] * imag - probe[m, 1] * real
                adds.append(obj_real * real + obj_imag * imag)
                adds.append(obj_real * imag - obj_imag * real)
            adds.append((obj_real * obj_real + obj_imag * obj_imag) * flag)
            for k in range(5):
                terms[k] = adds[k] if member == 0 else terms[k] + adds[k]
            for k, piece in enumerate((grad_real, grad_imag, light_buf[...] * flag)):
                turned = pltpu.roll(piece, shift, 1)
                grad[k, first, pl.ds(row, W), :] += jnp.where(keep, turned, 0.0)
                grad[k, second, pl.ds(row, W), :] += jnp.where(keep, 0.0, turned)
        for k in range(5):
            sums[k] += terms[k]

    def third_stage(turn):
        for member in range(BATCH):
            stacked = jnp.concatenate([back_buf[member, :256], back_buf[member]], axis=0)
            near = dot(on_left(2), stacked)
            real_hi, real_lo = split_two(near[:W])
            imag_hi, imag_lo = split_two(near[W:])
            for m in range(2):
                cut = slice(m * W, (m + 1) * W)
                near_buf[member, m] = jnp.concatenate(
                    [real_hi[:, cut], imag_hi[:, cut], real_lo[:, cut], imag_lo[:, cut]], axis=1
                )

    def scale(turn, far=None):
        for member in range(BATCH):
            slot, flag = member_slot(turn, member)
            far_real = far_buf[member, :W] if far is None else far[member][:W]
            far_imag = far_buf[member, W:] if far is None else far[member][W:]
            power = far_real * far_real + far_imag * far_imag
            model = jnp.maximum(power[:, :W] + power[:, W:], FLOOR_SQ)
            frame = intens[slot]
            ratio = frame * lax.rsqrt(jnp.maximum(frame * model, TINY))
            factor = (1.0 - ratio) * flag
            factor = jnp.concatenate([factor, factor], axis=1)
            real_hi, real_lo = split_two(far_real * factor)
            imag_hi, imag_lo = split_two(far_imag * factor)
            back_buf[member] = jnp.concatenate([real_hi, imag_hi, real_lo, imag_lo], axis=0)

    def second_stage(turn):
        for member in range(BATCH):
            stacked = jnp.concatenate([mid_buf[member, :256], mid_buf[member]], axis=0)
            far_buf[member] = dot(on_left(0), stacked)

    def first_stage(turn):
        ring = lax.bitwise_and(turn, RING - 1)
        rows = []
        for member in range(BATCH):
            slot, flag = member_slot(turn, member)
            row, first, second, shift = place(slot)
            back = lax.bitwise_and(128 - shift, 127)
            keep = lane >= shift
            patch = []
            for k in range(2):
                one = obj[k, first, pl.ds(row, W), :]
                two = obj[k, second, pl.ds(row, W), :]
                patch.append(pltpu.roll(jnp.where(keep, one, two), back, 1))
                patch_buf[ring, member, k] = patch[k]
            for m in range(2):
                real_hi, real_lo = split_two(probe[m, 0] * patch[0] - probe[m, 1] * patch[1])
                imag_hi, imag_lo = split_two(probe[m, 0] * patch[1] + probe[m, 1] * patch[0])
                rows.append(
                    jnp.concatenate([real_hi, imag_hi, real_lo, imag_lo, real_hi, imag_hi], axis=1)
                )
        mid = dot(jnp.concatenate(rows, axis=0), on_right(2))
        for member in range(BATCH):
            base = member * 2 * W
            real_hi, real_lo = split_two(
                jnp.concatenate([mid[base : base + W, :W], mid[base + W : base + 2 * W, :W]], axis=1)
            )
            imag_hi, imag_lo = split_two(
                jnp.concatenate([mid[base : base + W, W:], mid[base + W : base + 2 * W, W:]], axis=1)
            )
            mid_buf[member] = jnp.concatenate([real_hi, imag_hi, real_lo, imag_lo], axis=0)

    order = str(ORDER)
    lag = {}
    for before, now in zip(" 12345", "123456"):
        lag[now] = 0 if before == " " else lag[before] + (order.index(now) < order.index(before))

    def body(turn, carry):
        held = None
        for stage in order:
            at = turn - lag[stage]
            if stage == "1":
                first_stage(at)
            elif stage == "2":
                second_stage(at)
            elif stage == "3":
                scale(at)
            elif stage == "4":
                third_stage(at)
            elif stage == "5":
                held = last_product(at)
            else:
                last_adds(at, held)
        return carry

    lax.fori_loop(0, (own + BATCH - 1) // BATCH + lag["6"], body, 0)


def frames(places, obj, probe, intens, tables):
    vmem = pl.BlockSpec(memory_space=pltpu.VMEM)
    smem = pl.BlockSpec(memory_space=pltpu.SMEM)
    return pl.pallas_call(
        frames_kernel,
        out_shape=(
            jax.ShapeDtypeStruct((3, 3, EXT, W), jnp.float32),
            jax.ShapeDtypeStruct((5, W, W), jnp.float32),
        ),
        in_specs=[smem] + [vmem] * 4,
        out_specs=(vmem, vmem),
        scratch_shapes=[
            pltpu.VMEM((RING, BATCH, 2, W, W), jnp.float32),
            pltpu.VMEM((BATCH, 4 * W, 2 * W), jnp.bfloat16),
            pltpu.VMEM((BATCH, 2 * W, 2 * W), jnp.float32),
            pltpu.VMEM((BATCH, 4 * W, 2 * W), jnp.bfloat16),
            pltpu.VMEM((BATCH, 2, W, 4 * W), jnp.bfloat16),
            pltpu.VMEM((W, W), jnp.float32),
        ],
        compiler_params=pltpu.CompilerParams(vmem_limit_bytes=FRAMES_VMEM),
        cost_estimate=pl.CostEstimate(flops=9_600_000_000, bytes_accessed=10_000_000, transcendentals=0),
        name="frames",
    )(places, obj, probe, intens, tables)


def own_place():
    row = lax.axis_index("row")
    col = lax.axis_index("col")
    core = row % 2
    z_hi = (row // 2) % 4
    x = row // 8
    y = col // 2
    z_lo = col % 2
    return row, col, core, x, y, z_hi, z_lo


PLANES = (2, 0, 1)


def spread_kernel(fold, halo, *refs):
    refs = list(refs)
    take = lambda n: [refs.pop(0) for _ in range(n)]
    if fold:
        obj_in, probe_in, grad, sums = take(4)
    else:
        (obj_in,) = take(1)
    (obj_out,) = take(1)
    if fold:
        if halo:
            (tile_out,) = take(1)
        (probe_out,) = take(1)
        (pair_buf, rs_src, rs_buf, z_src, z_buf, ag_buf, ag_pair, fold_r, mid, mid_s, mid_r, edge_s, edge_r) = take(13)
        (pair_ss, pair_rs, rs_ss, rs_rs, z_ss, z_rs, ag_ss, ag_rs, agp_ss, agp_rs) = take(10)
        (fr_ss, fr_rs, fm_ss, fm_rs, fe_ss, fe_rs) = take(6)
    if halo:
        halo_cs, halo_c, halo_r, corner_r, hc_ss, hc_rs, hr_ss, hr_rs, ho_ss, ho_rs = take(10)

    row, col, core, x, y, z_hi, z_lo = own_place()
    plane = x * 4 + y
    z = z_hi * 2 + z_lo
    up = (lax.rem(row + N_ROW - 1, N_ROW), col)
    down = (lax.rem(row + 1, N_ROW), col)
    left = (row, lax.rem(col + N_COL - 1, N_COL))
    right = (row, lax.rem(col + 1, N_COL))
    pair = (row + 1 - 2 * core, col)
    has_up = row > 0
    has_down = row < N_ROW - 1
    has_left = col > 0
    has_right = col < N_COL - 1

    def turn(value, size):
        return jnp.where(value >= size, value - size, value)

    def plane_mate(step):
        far_x = turn(x + step // 4, 4)
        far_y = turn(y + step % 4, 4)
        return far_x * 4 + far_y, ((far_x * 4 + z_hi) * 2 + core, far_y * 2 + z_lo)

    def plane_source(step):
        return turn(x + (4 - step // 4) % 4, 4) * 4 + turn(y + (4 - step % 4) % 4, 4)

    def z_mate(step):
        other = turn(z + step, N_Z)
        return other, ((x * 4 + other // 2) * 2 + core, y * 2 + other % 2)

    def copy(src, dst, ss, rs, device):
        return pltpu.make_async_remote_copy(
            src_ref=src, dst_ref=dst, send_sem=ss, recv_sem=rs, device_id=device, device_id_type=MESH
        )

    barrier = pltpu.get_barrier_semaphore()

    def greet(device):
        pl.semaphore_signal(barrier, inc=1, device_id=device, device_id_type=MESH)

    for device in (up, down, left, right):
        greet(device)
    greeted = 4
    if fold:
        greet(pair)
        for step in range(1, N_PLANE):
            greet(plane_mate(step)[1])
        for step in range(1, N_Z):
            greet(z_mate(step)[1])
        greeted += 1 + N_PLANE - 1 + N_Z - 1
    pl.semaphore_wait(barrier, greeted)

    def pick(first, second):
        shape = jnp.shape(first) or jnp.shape(second)
        return jnp.where(lax.broadcasted_iota(jnp.int32, shape, 1) < MARGIN, first, second)

    def half(value):
        return pltpu.roll(value, MARGIN, 1)

    def rs_copy(step):
        other, device = plane_mate(step)
        return copy(rs_src.at[other], rs_buf.at[plane], rs_ss.at[step], rs_rs.at[step], device)

    def rs_arrival(step):
        other = plane_source(step)
        return copy(rs_src.at[other], rs_buf.at[other], rs_ss.at[step], rs_rs.at[step], up)

    def z_copy(step):
        return copy(z_src, z_buf.at[z], z_ss.at[step], z_rs.at[step], z_mate(step)[1])

    def z_arrival(step):
        other = turn(z + N_Z - step, N_Z)
        return copy(z_src, z_buf.at[other], z_ss.at[step], z_rs.at[step], up)

    def ag_copy(step):
        return copy(ag_buf.at[plane], ag_buf.at[plane], ag_ss.at[step], ag_rs.at[step], plane_mate(step)[1])

    def ag_arrival(step):
        other = plane_source(step)
        return copy(ag_buf.at[other], ag_buf.at[other], ag_ss.at[step], ag_rs.at[step], up)

    def each(count, act):
        for step in range(1, count):
            act(step)

    sent = []

    def go(*copies):
        for one in copies:
            one.start()
            sent.append(one)
        return copies

    def land(copies):
        for one in copies:
            one.wait_recv()

    def both(src, dst, ss, rs, at, first, second):
        return go(
            copy(src(0), dst(0), ss.at[2 * at], rs.at[2 * at], first),
            copy(src(1), dst(1), ss.at[2 * at + 1], rs.at[2 * at + 1], second),
        )

    def tie(upper, lower):
        return pick(half(upper), lower), pick(upper, half(lower))

    if fold:
        pair_copies = go(
            copy(sums.at[pl.ds(2 * (1 - core), 2)], pair_buf.at[pl.ds(0, 2)], pair_ss.at[0], pair_rs.at[0], pair),
            copy(sums.at[pl.ds(4, 1)], pair_buf.at[pl.ds(2, 1)], pair_ss.at[1], pair_rs.at[1], pair),
        )
        fr_copies = {}
        for k in PLANES:
            fr_copies[k] = both(
                lambda i: grad.at[k, :, pl.ds(i * (TILE + MARGIN), MARGIN)],
                lambda i: fold_r.at[i, k], fr_ss, fr_rs, k, up, down,
            )
        for k in PLANES:
            packs = tie(grad[k, 2, 2 * MARGIN : 3 * MARGIN], grad[k, 2, 3 * MARGIN : 4 * MARGIN])
            for i in range(2):
                mid_s[i, k] = packs[i]
        fm_copies = both(lambda i: mid_s.at[i], lambda i: mid_r.at[i], fm_ss, fm_rs, 0, left, right)

        land(pair_copies)
        for k in range(3):
            own = sums[4] if k == 2 else sums[2 * core + k]
            rs_src[:, k] = own + pair_buf[k]
        each(N_PLANE, lambda s: rs_copy(s).start())
        rs_buf[plane] = rs_src[plane]

        fe_copies = {}

        def fold_rows(k):
            land(fr_copies[k])
            mid[k, :, :MARGIN] = grad[k, :, MARGIN : 2 * MARGIN] + jnp.where(has_up, fold_r[1, k], 0.0)
            mid[k, :, MARGIN:] = grad[k, :, TILE : TILE + MARGIN] + jnp.where(has_down, fold_r[0, k], 0.0)
            packs = tie(mid[k, 2, :MARGIN], mid[k, 2, MARGIN:])
            for i in range(2):
                edge_s[i, k] = packs[i]
            fe_copies[k] = both(
                lambda i: edge_s.at[i, k], lambda i: edge_r.at[i, k], fe_ss, fe_rs, k, left, right
            )

        fold_rows(PLANES[0])
        fold_rows(PLANES[1])
        each(N_PLANE, lambda s: rs_arrival(s).wait_recv())
        total = rs_buf[0]
        for other in range(1, N_PLANE):
            total = total + rs_buf[other]
        z_src[...] = total
        z_buf[z] = total
        each(N_Z, lambda s: z_copy(s).start())
        fold_rows(PLANES[2])
        land(fm_copies)

        def block_of(k, block):
            if block in (0, 3):
                start = 0 if block == 0 else MARGIN
                base = [mid[k, part, start : start + MARGIN] for part in range(2)]
                got = edge_r
            else:
                start = MARGIN + block * MARGIN
                base = [grad[k, part, start : start + MARGIN] for part in range(2)]
                got = mid_r
            from_right = jnp.where(has_right, got[0, k], 0.0)
            from_left = jnp.where(has_left, got[1, k], 0.0)
            if block in (0, 1):
                from_right = half(from_right)
            else:
                from_left = half(from_left)
            return base[0] + pick(from_left, 0.0), base[1] + pick(0.0, from_right)

        land(fe_copies[2])
        weights = [[1.0 / (one + OBJECT_REG) for one in block_of(2, block)] for block in range(4)]

        def update(k):
            land(fe_copies[k])
            for block in range(4):
                parts = block_of(k, block)
                start = block * MARGIN
                for part in range(2):
                    step = parts[part] * weights[block][part]
                    cut = slice(part * W, (part + 1) * W)
                    if halo:
                        new = obj_in[k, part, MARGIN + start : 2 * MARGIN + start] - step
                        obj_out[k, part, MARGIN + start : 2 * MARGIN + start] = new
                        tile_out[k, start : start + MARGIN, cut] = new
                    else:
                        obj_out[k, start : start + MARGIN, cut] = step
    else:

        def update(k):
            for part in range(2):
                obj_out[k, part, MARGIN : MARGIN + TILE] = obj_in[k, :, part * W : (part + 1) * W]

    hc_copies = {}
    hr_copies = {}
    ho_copies = {}

    def send_halo(k):
        first = tie(obj_out[k, 1, MARGIN : MARGIN + W], obj_out[k, 1, MARGIN + W : MARGIN + TILE])[0]
        last = tie(obj_out[k, 0, MARGIN : MARGIN + W], obj_out[k, 0, MARGIN + W : MARGIN + TILE])[1]
        halo_cs[0, k] = last
        halo_cs[1, k] = first
        hc_copies[k] = both(lambda i: halo_cs.at[i, k], lambda i: halo_c.at[i, k], hc_ss, hc_rs, k, left, right)
        hr_copies[k] = both(
            lambda i: obj_out.at[k, pl.ds(0, 2), pl.ds(MARGIN + i * (TILE - MARGIN), MARGIN)],
            lambda i: halo_r.at[i, k], hr_ss, hr_rs, k, up, down,
        )

    update(0)
    if halo:
        send_halo(0)
    if fold:
        each(N_Z, lambda s: z_arrival(s).wait_recv())
        total = z_buf[0]
        for other in range(1, N_Z):
            total = total + z_buf[other]
        weight = 1.0 / (total[2] + PROBE_REG)
        for k in range(2):
            step = total[k] * weight
            ag_buf[plane, k] = probe_in[core, k, plane] - step if halo else step
        each(N_PLANE, lambda s: ag_copy(s).start())
    update(1)
    if halo:
        send_halo(1)

        def margins(k):
            land(hc_copies[k])
            from_right = jnp.where(has_right, halo_c[0, k], 0.0)
            from_left = jnp.where(has_left, halo_c[1, k], 0.0)
            obj_out[k, 2, MARGIN : MARGIN + W] = pick(from_right, half(from_left))
            obj_out[k, 2, MARGIN + W : MARGIN + TILE] = pick(half(from_right), from_left)
            ho_copies[k] = both(
                lambda i: obj_out.at[k, 2, pl.ds(MARGIN + i * (TILE - MARGIN), MARGIN)],
                lambda i: corner_r.at[i, k], ho_ss, ho_rs, k, up, down,
            )

        margins(0)
        margins(1)

    if fold:
        each(N_PLANE, lambda s: ag_arrival(s).wait_recv())
        (agp,) = go(copy(ag_buf, ag_pair, agp_ss.at[0], agp_rs.at[0], pair))
        for k in range(2):
            probe_out[core, k] = ag_buf[:, k]

    if halo:
        for k in range(2):
            land(hr_copies[k])
            obj_out[k, :2, TILE + MARGIN :] = jnp.where(has_down, halo_r[0, k], 0.0)
            obj_out[k, :2, :MARGIN] = jnp.where(has_up, halo_r[1, k], 0.0)
        for k in range(2):
            land(ho_copies[k])
            obj_out[k, 2, TILE + MARGIN :] = jnp.where(has_down, corner_r[0, k], 0.0)
            obj_out[k, 2, :MARGIN] = jnp.where(has_up, corner_r[1, k], 0.0)

    if fold:
        land([agp])
        for k in range(2):
            probe_out[1 - core, k] = ag_pair[:, k]
    for one in sent:
        one.wait_send()
    if fold:
        each(N_PLANE, lambda s: rs_copy(s).wait_send())
        each(N_Z, lambda s: z_copy(s).wait_send())
        each(N_PLANE, lambda s: ag_copy(s).wait_send())


def spread(fold, halo, number, *operands):
    vmem = pl.BlockSpec(memory_space=pltpu.VMEM)
    dma = pltpu.SemaphoreType.DMA
    f32 = jnp.float32
    outs = []
    if halo:
        outs.append(jax.ShapeDtypeStruct((2, 3, EXT, W), f32))
    if fold or not halo:
        outs.append(jax.ShapeDtypeStruct((2, TILE, TILE), f32))
    scratch = []
    if fold:
        outs.append(jax.ShapeDtypeStruct((2, 2, 16, 8, W), f32))
        scratch += [
            pltpu.VMEM((3, 16, 8, W), f32),
            pltpu.VMEM((16, 3, 8, W), f32),
            pltpu.VMEM((16, 3, 8, W), f32),
            pltpu.VMEM((3, 8, W), f32),
            pltpu.VMEM((8, 3, 8, W), f32),
            pltpu.VMEM((16, 2, 8, W), f32),
            pltpu.VMEM((16, 2, 8, W), f32),
            pltpu.VMEM((2, 3, 3, MARGIN, W), f32),
            pltpu.VMEM((3, 3, 2 * MARGIN, W), f32),
            pltpu.VMEM((2, 3, MARGIN, W), f32),
            pltpu.VMEM((2, 3, MARGIN, W), f32),
            pltpu.VMEM((2, 3, MARGIN, W), f32),
            pltpu.VMEM((2, 3, MARGIN, W), f32),
            dma((2,)), dma((2,)), dma((16,)), dma((16,)), dma((8,)), dma((8,)), dma((16,)), dma((16,)),
            dma((1,)), dma((1,)), dma((6,)), dma((6,)), dma((2,)), dma((2,)), dma((6,)), dma((6,)),
        ]
    if halo:
        scratch += [
            pltpu.VMEM((2, 2, W, W), f32),
            pltpu.VMEM((2, 2, W, W), f32),
            pltpu.VMEM((2, 2, 2, MARGIN, W), f32),
            pltpu.VMEM((2, 2, MARGIN, W), f32),
            dma((4,)), dma((4,)), dma((4,)), dma((4,)), dma((4,)), dma((4,)),
        ]
    return pl.pallas_call(
        functools.partial(spread_kernel, fold, halo),
        out_shape=tuple(outs),
        in_specs=[vmem] * len(operands),
        out_specs=(vmem,) * len(outs),
        scratch_shapes=scratch,
        compiler_params=pltpu.CompilerParams(
            collective_id=number, has_side_effects=True, vmem_limit_bytes=SPREAD_VMEM
        ),
        cost_estimate=pl.CostEstimate(flops=0, bytes_accessed=40_000_000, transcendentals=0),
        name="spread" + str(number),
    )(*operands)


def per_device(object_slab, probe_modes, intensities, positions, live_counts):
    tables = jnp.asarray(dft_parts())
    where = jnp.concatenate([positions.reshape(2 * SLOTS), live_counts.reshape(N_ROW * N_COL)])
    intens = intensities.reshape(SLOTS, W, W)
    probe = probe_modes
    (current,) = spread(False, True, 0, object_slab)
    for sweep in range(ITERS):
        grad, sums = frames(where, current, probe, intens, tables)
        last = sweep == ITERS - 1
        outs = spread(
            True, not last, sweep + 1,
            current, probe.reshape(2, 2, 16, 8, W), grad, sums.reshape(5, 16, 8, W),
        )
        if last:
            return tile - outs[0], probe - outs[1].reshape(2, 2, W, W)
        current, tile, probe = outs
        probe = probe.reshape(2, 2, W, W)


def solution(mesh):
    return jax.shard_map(
        per_device,
        mesh=mesh,
        in_specs=(
            P(None, "row", "col"),
            P(),
            P("row", "col", None, None, None),
            P("row", "col", None, None),
            P(),
        ),
        out_specs=(P(None, "row", "col"), P()),
        check_vma=False,
    )
```

```python
import functools

import jax
import jax.numpy as jnp
import ml_dtypes
import numpy as np
from jax import lax
from jax.experimental import pallas as pl
from jax.experimental.pallas import tpu as pltpu
from jax.sharding import PartitionSpec as P

ITERS = 2
W = 128
MARGIN = 64
TILE = 256
EXT = TILE + 2 * MARGIN
SLOTS = 24
BATCH = 1
RING = 8
UNROLL = 3
ORDER = 321546
OBJECT_REG = 1.0
PROBE_REG = 1.0
FLOOR_SQ = 0.0625
TINY = 1e-36
N_ROW = 32
N_COL = 8
N_PLANE = 16
N_Z = 8
FRAMES_VMEM = 20 * 1024 * 1024
SPREAD_VMEM = 16 * 1024 * 1024
MESH = pl.DeviceIdType.MESH
NEAR = ((-1, -1), (-1, 0), (-1, 1), (0, -1), (0, 1), (1, -1), (1, 0), (1, 1))
CHUNK = 8
ROWS, COLS, COUNTS = 8, 9, 10


def dft_parts():
    counter = np.arange(W)
    angles = (counter[:, None] * counter[None, :] % W) * (2.0 * np.pi / W)
    cosine = np.cos(angles) / np.sqrt(W)
    sine = np.sin(angles) / np.sqrt(W)
    fore = np.block([[cosine, sine], [-sine, cosine]])
    back = np.block([[cosine, -sine], [sine, cosine]])

    def split(table):
        high = table.astype(np.float32).astype(ml_dtypes.bfloat16)
        low = (table - high.astype(np.float64)).astype(np.float32).astype(ml_dtypes.bfloat16)
        return high, low

    fore_hi, fore_lo = split(fore)
    back_hi, back_lo = split(back)
    return np.stack([fore_hi, fore_lo, back_hi, back_lo])


def split_two(value):
    high = value.astype(jnp.bfloat16)
    low = (value - high.astype(jnp.float32)).astype(jnp.bfloat16)
    return high, low


def dot(left, right):
    return jnp.dot(left, right, preferred_element_type=jnp.float32)


def frames_kernel(
    spots, obj, probe, intens, tables,
    grad, sums, weight, patch_buf, mid_buf, far_buf, back_buf, near_buf, light_buf, illum, listed,
):
    grad[...] = jnp.zeros_like(grad)
    sums[...] = jnp.zeros_like(sums)
    for buffer in (patch_buf, mid_buf, far_buf, back_buf, near_buf):
        buffer[...] = jnp.zeros_like(buffer)
    lighting = probe[0, 0] * probe[0, 0] + probe[0, 1] * probe[0, 1]
    light_buf[...] = lighting + probe[1, 0] * probe[1, 0] + probe[1, 1] * probe[1, 1]
    own = spots[COUNTS, len(NEAR)]

    def on_left(high):
        return jnp.concatenate([tables[high], tables[high + 1], tables[high]], axis=1)

    def on_right(high):
        return jnp.concatenate([tables[high], tables[high], tables[high + 1]], axis=0)

    lane = lax.broadcasted_iota(jnp.int32, (W, W), 1)

    def place(slot):
        row = spots[ROWS, slot]
        col = spots[COLS, slot]
        col = jnp.where(col < 0, col + EXT, col)
        first = lax.shift_right_logical(col, 7)
        shift = lax.bitwise_and(col, 127)
        second = jnp.where(first == 2, 0, first + 1)
        return row, first, second, shift

    def member_slot(turn, member):
        slot = turn * BATCH + member
        flag = jnp.where(jnp.logical_and(slot >= 0, slot < own), 1.0, 0.0).astype(jnp.float32)
        return jnp.clip(slot, 0, SLOTS - 1), flag

    def last_product(turn):
        halves = []
        for member in range(BATCH):
            for m in range(2):
                halves.append(jnp.concatenate([near_buf[member, m], near_buf[member, m, :, : 2 * W]], axis=1))
        return dot(jnp.concatenate(halves, axis=0), on_right(0))

    def last_adds(turn, resid):
        ring = lax.bitwise_and(turn, RING - 1)
        terms = [None] * 5
        for member in range(BATCH):
            slot, flag = member_slot(turn, member)
            row, first, second, shift = place(slot)
            keep = lane >= shift
            obj_real = patch_buf[ring, member, 0]
            obj_imag = patch_buf[ring, member, 1]
            grad_real = 0.0
            grad_imag = 0.0
            adds = []
            for m in range(2):
                base = (member * 2 + m) * W
                real = resid[base : base + W, :W]
                imag = resid[base : base + W, W:]
                grad_real = grad_real + probe[m, 0] * real + probe[m, 1] * imag
                grad_imag = grad_imag + probe[m, 0] * imag - probe[m, 1] * real
                adds.append(obj_real * real + obj_imag * imag)
                adds.append(obj_real * imag - obj_imag * real)
            adds.append((obj_real * obj_real + obj_imag * obj_imag) * flag)
            for k in range(5):
                terms[k] = adds[k] if member == 0 else terms[k] + adds[k]
            for k, piece in enumerate((grad_real, grad_imag)):
                turned = pltpu.roll(piece, shift, 1)
                grad[k, first, pl.ds(row, W), :] += jnp.where(keep, turned, 0.0)
                grad[k, second, pl.ds(row, W), :] += jnp.where(keep, 0.0, turned)
            turned = pltpu.roll(light_buf[...] * flag, shift, 1)
            at = jnp.where(first == 2, 0, first + 1)
            illum[at, pl.ds(row + MARGIN, W), :] += jnp.where(keep, turned, 0.0)
            illum[at + 1, pl.ds(row + MARGIN, W), :] += jnp.where(keep, 0.0, turned)
        for k in range(5):
            sums[k] += terms[k]

    def third_stage(turn):
        for member in range(BATCH):
            stacked = jnp.concatenate([back_buf[member, :256], back_buf[member]], axis=0)
            near = dot(on_left(2), stacked)
            real_hi, real_lo = split_two(near[:W])
            imag_hi, imag_lo = split_two(near[W:])
            for m in range(2):
                cut = slice(m * W, (m + 1) * W)
                near_buf[member, m] = jnp.concatenate(
                    [real_hi[:, cut], imag_hi[:, cut], real_lo[:, cut], imag_lo[:, cut]], axis=1
                )

    def scale(turn, far=None):
        for member in range(BATCH):
            slot, flag = member_slot(turn, member)
            far_real = far_buf[member, :W] if far is None else far[member][:W]
            far_imag = far_buf[member, W:] if far is None else far[member][W:]
            power = far_real * far_real + far_imag * far_imag
            model = jnp.maximum(power[:, :W] + power[:, W:], FLOOR_SQ)
            frame = intens[slot]
            ratio = frame * lax.rsqrt(jnp.maximum(frame * model, TINY))
            factor = (1.0 - ratio) * flag
            factor = jnp.concatenate([factor, factor], axis=1)
            real_hi, real_lo = split_two(far_real * factor)
            imag_hi, imag_lo = split_two(far_imag * factor)
            back_buf[member] = jnp.concatenate([real_hi, imag_hi, real_lo, imag_lo], axis=0)

    def second_stage(turn):
        for member in range(BATCH):
            stacked = jnp.concatenate([mid_buf[member, :256], mid_buf[member]], axis=0)
            far_buf[member] = dot(on_left(0), stacked)

    def first_stage(turn):
        ring = lax.bitwise_and(turn, RING - 1)
        rows = []
        for member in range(BATCH):
            slot, flag = member_slot(turn, member)
            row, first, second, shift = place(slot)
            back = lax.bitwise_and(128 - shift, 127)
            keep = lane >= shift
            patch = []
            for k in range(2):
                one = obj[k, first, pl.ds(row, W), :]
                two = obj[k, second, pl.ds(row, W), :]
                patch.append(pltpu.roll(jnp.where(keep, one, two), back, 1))
                patch_buf[ring, member, k] = patch[k]
            for m in range(2):
                real_hi, real_lo = split_two(probe[m, 0] * patch[0] - probe[m, 1] * patch[1])
                imag_hi, imag_lo = split_two(probe[m, 0] * patch[1] + probe[m, 1] * patch[0])
                rows.append(
                    jnp.concatenate([real_hi, imag_hi, real_lo, imag_lo, real_hi, imag_hi], axis=1)
                )
        mid = dot(jnp.concatenate(rows, axis=0), on_right(2))
        for member in range(BATCH):
            base = member * 2 * W
            real_hi, real_lo = split_two(
                jnp.concatenate([mid[base : base + W, :W], mid[base + W : base + 2 * W, :W]], axis=1)
            )
            imag_hi, imag_lo = split_two(
                jnp.concatenate([mid[base : base + W, W:], mid[base + W : base + 2 * W, W:]], axis=1)
            )
            mid_buf[member] = jnp.concatenate([real_hi, imag_hi, real_lo, imag_lo], axis=0)

    illum[...] = jnp.zeros_like(illum)
    held_count = jnp.int32(0)
    for near in range(len(NEAR)):
        there = spots[COUNTS, near]

        def gather(chunk, held):
            for k in range(CHUNK):
                slot = chunk * CHUNK + k
                packed = spots[near, slot]
                listed[held] = packed
                fits = jnp.logical_and(packed > 0, slot < there)
                held = held + jnp.where(fits, 1, 0)
            return held

        held_count = lax.fori_loop(0, (there + CHUNK - 1) // CHUNK, gather, held_count)

    def shine(step, carry):
        for k in range(2):
            entry = 2 * step + k
            live = entry < held_count
            packed = jnp.where(live, listed[jnp.where(live, entry, 0)], 1025)
            flag = jnp.where(live, 1.0, 0.0).astype(jnp.float32)
            row = lax.shift_right_logical(packed, 10)
            col = lax.bitwise_and(packed, 1023)
            first = lax.shift_right_logical(col, 7)
            shift = lax.bitwise_and(col, 127)
            keep = lane >= shift
            turned = pltpu.roll(light_buf[...] * flag, shift, 1)
            illum[first, pl.ds(row, W), :] += jnp.where(keep, turned, 0.0)
            illum[first + 1, pl.ds(row, W), :] += jnp.where(keep, 0.0, turned)
        return carry

    lax.fori_loop(0, (held_count + 1) // 2, shine, 0)

    order = str(ORDER)
    lag = {}
    for before, now in zip(" 12345", "123456"):
        lag[now] = 0 if before == " " else lag[before] + (order.index(now) < order.index(before))

    def body(turn, carry):
        held = None
        for stage in order:
            at = turn - lag[stage]
            if stage == "1":
                first_stage(at)
            elif stage == "2":
                second_stage(at)
            elif stage == "3":
                scale(at)
            elif stage == "4":
                third_stage(at)
            elif stage == "5":
                held = last_product(at)
            else:
                last_adds(at, held)
        return carry

    turns = (own + BATCH - 1) // BATCH + lag["6"]

    def several(step, carry):
        for k in range(UNROLL):
            body(step * UNROLL + k, 0)
        return carry

    lax.fori_loop(0, (turns + UNROLL - 1) // UNROLL, several, 0)
    for part in range(2):
        weight[part] = 1.0 / (illum[part + 1, W : W + TILE, :] + OBJECT_REG)


def frames(spots, obj, probe, intens, tables):
    vmem = pl.BlockSpec(memory_space=pltpu.VMEM)
    smem = pl.BlockSpec(memory_space=pltpu.SMEM)
    return pl.pallas_call(
        frames_kernel,
        out_shape=(
            jax.ShapeDtypeStruct((2, 3, EXT, W), jnp.float32),
            jax.ShapeDtypeStruct((5, W, W), jnp.float32),
            jax.ShapeDtypeStruct((2, TILE, W), jnp.float32),
        ),
        in_specs=[smem] + [vmem] * 4,
        out_specs=(vmem, vmem, vmem),
        scratch_shapes=[
            pltpu.VMEM((RING, BATCH, 2, W, W), jnp.float32),
            pltpu.VMEM((BATCH, 4 * W, 2 * W), jnp.bfloat16),
            pltpu.VMEM((BATCH, 2 * W, 2 * W), jnp.float32),
            pltpu.VMEM((BATCH, 4 * W, 2 * W), jnp.bfloat16),
            pltpu.VMEM((BATCH, 2, W, 4 * W), jnp.bfloat16),
            pltpu.VMEM((W, W), jnp.float32),
            pltpu.VMEM((4, 2 * TILE, W), jnp.float32),
            pltpu.SMEM((len(NEAR) * SLOTS + CHUNK,), jnp.int32),
        ],
        compiler_params=pltpu.CompilerParams(vmem_limit_bytes=FRAMES_VMEM),
        cost_estimate=pl.CostEstimate(flops=9_600_000_000, bytes_accessed=10_000_000, transcendentals=0),
        name="frames",
    )(spots, obj, probe, intens, tables)


def own_place():
    row = lax.axis_index("row")
    col = lax.axis_index("col")
    core = row % 2
    z_hi = (row // 2) % 4
    x = row // 8
    y = col // 2
    z_lo = col % 2
    return row, col, core, x, y, z_hi, z_lo


def spread_kernel(fold, halo, *refs):
    refs = list(refs)
    take = lambda n: [refs.pop(0) for _ in range(n)]
    if fold:
        obj_in, probe_in, grad, sums, weight_in = take(5)
    else:
        obj_in, places_in = take(2)
    (obj_out,) = take(1)
    if not fold:
        (spots_out,) = take(1)
        line_buf, spots_buf, spots_ss, spots_rs = take(4)
    if fold:
        if halo:
            (tile_out,) = take(1)
        (probe_out,) = take(1)
        (pair_buf, rs_src, rs_buf, z_src, z_buf, ag_buf, ag_pair, fold_r, mid, mid_s, mid_r, edge_s, edge_r) = take(13)
        (pair_ss, pair_rs, rs_ss, rs_rs, z_ss, z_rs, ag_ss, ag_rs, agp_ss, agp_rs) = take(10)
        (fr_ss, fr_rs, fm_ss, fm_rs, fe_ss, fe_rs) = take(6)
    if halo:
        halo_cs, halo_c, halo_r, corner_r, hc_ss, hc_rs, hr_ss, hr_rs, ho_ss, ho_rs = take(10)

    row, col, core, x, y, z_hi, z_lo = own_place()
    plane = x * 4 + y
    z = z_hi * 2 + z_lo
    up = (lax.rem(row + N_ROW - 1, N_ROW), col)
    down = (lax.rem(row + 1, N_ROW), col)
    left = (row, lax.rem(col + N_COL - 1, N_COL))
    right = (row, lax.rem(col + 1, N_COL))
    pair = (row + 1 - 2 * core, col)
    has_up = row > 0
    has_down = row < N_ROW - 1
    has_left = col > 0
    has_right = col < N_COL - 1

    def turn(value, size):
        return jnp.where(value >= size, value - size, value)

    def plane_mate(step):
        far_x = turn(x + step // 4, 4)
        far_y = turn(y + step % 4, 4)
        return far_x * 4 + far_y, ((far_x * 4 + z_hi) * 2 + core, far_y * 2 + z_lo)

    def plane_source(step):
        return turn(x + (4 - step // 4) % 4, 4) * 4 + turn(y + (4 - step % 4) % 4, 4)

    def z_mate(step):
        other = turn(z + step, N_Z)
        return other, ((x * 4 + other // 2) * 2 + core, y * 2 + other % 2)

    def copy(src, dst, ss, rs, device):
        return pltpu.make_async_remote_copy(
            src_ref=src, dst_ref=dst, send_sem=ss, recv_sem=rs, device_id=device, device_id_type=MESH
        )

    barrier = pltpu.get_barrier_semaphore()

    def greet(device):
        pl.semaphore_signal(barrier, inc=1, device_id=device, device_id_type=MESH)

    for device in (up, down, left, right):
        greet(device)
    greeted = 4
    if fold:
        greet(pair)
        for step in range(1, N_PLANE):
            greet(plane_mate(step)[1])
        for step in range(1, N_Z):
            greet(z_mate(step)[1])
        greeted += 1 + N_PLANE - 1 + N_Z - 1
    pl.semaphore_wait(barrier, greeted)

    def pick(first, second):
        shape = jnp.shape(first) or jnp.shape(second)
        return jnp.where(lax.broadcasted_iota(jnp.int32, shape, 1) < MARGIN, first, second)

    def half(value):
        return pltpu.roll(value, MARGIN, 1)

    def rs_copy(step):
        other, device = plane_mate(step)
        return copy(rs_src.at[other], rs_buf.at[plane], rs_ss.at[step], rs_rs.at[step], device)

    def rs_arrival(step):
        other = plane_source(step)
        return copy(rs_src.at[other], rs_buf.at[other], rs_ss.at[step], rs_rs.at[step], up)

    def z_copy(step):
        return copy(z_src, z_buf.at[z], z_ss.at[step], z_rs.at[step], z_mate(step)[1])

    def z_arrival(step):
        other = turn(z + N_Z - step, N_Z)
        return copy(z_src, z_buf.at[other], z_ss.at[step], z_rs.at[step], up)

    def ag_copy(step):
        return copy(ag_buf.at[plane], ag_buf.at[plane], ag_ss.at[step], ag_rs.at[step], plane_mate(step)[1])

    def ag_arrival(step):
        other = plane_source(step)
        return copy(ag_buf.at[other], ag_buf.at[other], ag_ss.at[step], ag_rs.at[step], up)

    def each(count, act):
        for step in range(1, count):
            act(step)

    sent = []

    def go(*copies):
        for one in copies:
            one.start()
            sent.append(one)
        return copies

    def land(copies):
        for one in copies:
            one.wait_recv()

    def both(src, dst, ss, rs, at, first, second):
        return go(
            copy(src(0), dst(0), ss.at[2 * at], rs.at[2 * at], first),
            copy(src(1), dst(1), ss.at[2 * at + 1], rs.at[2 * at + 1], second),
        )

    def tie(upper, lower):
        return pick(half(upper), lower), pick(upper, half(lower))

    if fold:
        pair_copies = go(
            copy(sums.at[pl.ds(2 * (1 - core), 2)], pair_buf.at[pl.ds(0, 2)], pair_ss.at[0], pair_rs.at[0], pair),
            copy(sums.at[pl.ds(4, 1)], pair_buf.at[pl.ds(2, 1)], pair_ss.at[1], pair_rs.at[1], pair),
        )
        fr_copies = {}
        for k in range(2):
            fr_copies[k] = both(
                lambda i: grad.at[k, :, pl.ds(i * (TILE + MARGIN), MARGIN)],
                lambda i: fold_r.at[i, k], fr_ss, fr_rs, k, up, down,
            )
        for k in range(2):
            packs = tie(grad[k, 2, 2 * MARGIN : 3 * MARGIN], grad[k, 2, 3 * MARGIN : 4 * MARGIN])
            for i in range(2):
                mid_s[i, k] = packs[i]
        fm_copies = both(lambda i: mid_s.at[i], lambda i: mid_r.at[i], fm_ss, fm_rs, 0, left, right)

        land(pair_copies)
        for k in range(3):
            own = sums[4] if k == 2 else sums[2 * core + k]
            rs_src[:, k] = own + pair_buf[k]
        each(N_PLANE, lambda s: rs_copy(s).start())
        rs_buf[plane] = rs_src[plane]

        fe_copies = {}

        def fold_rows(k):
            land(fr_copies[k])
            mid[k, :, :MARGIN] = grad[k, :, MARGIN : 2 * MARGIN] + jnp.where(has_up, fold_r[1, k], 0.0)
            mid[k, :, MARGIN:] = grad[k, :, TILE : TILE + MARGIN] + jnp.where(has_down, fold_r[0, k], 0.0)
            packs = tie(mid[k, 2, :MARGIN], mid[k, 2, MARGIN:])
            for i in range(2):
                edge_s[i, k] = packs[i]
            fe_copies[k] = both(
                lambda i: edge_s.at[i, k], lambda i: edge_r.at[i, k], fe_ss, fe_rs, k, left, right
            )

        def block_of(k, block):
            if block in (0, 3):
                start = 0 if block == 0 else MARGIN
                base = [mid[k, part, start : start + MARGIN] for part in range(2)]
                got = edge_r
            else:
                start = MARGIN + block * MARGIN
                base = [grad[k, part, start : start + MARGIN] for part in range(2)]
                got = mid_r
            from_right = jnp.where(has_right, got[0, k], 0.0)
            from_left = jnp.where(has_left, got[1, k], 0.0)
            if block in (0, 1):
                from_right = half(from_right)
            else:
                from_left = half(from_left)
            return base[0] + pick(from_left, 0.0), base[1] + pick(0.0, from_right)

        def update(k, blocks):
            for block in blocks:
                parts = block_of(k, block)
                start = block * MARGIN
                for part in range(2):
                    step = parts[part] * weight_in[part, start : start + MARGIN]
                    cut = slice(part * W, (part + 1) * W)
                    if halo:
                        new = obj_in[k, part, MARGIN + start : 2 * MARGIN + start] - step
                        obj_out[k, part, MARGIN + start : 2 * MARGIN + start] = new
                        tile_out[k, start : start + MARGIN, cut] = new
                    else:
                        obj_out[k, start : start + MARGIN, cut] = step
    else:
        for k in range(2):
            for part in range(2):
                obj_out[k, part, MARGIN : MARGIN + TILE] = obj_in[k, :, part * W : (part + 1) * W]

    hc_copies = {}
    hr_copies = {}
    ho_copies = {}

    def send_cols(k, edge):
        one, two = (MARGIN, TILE) if edge else (2 * MARGIN, 3 * MARGIN)
        at = 2 * k + edge
        first = tie(obj_out[k, 1, one : one + MARGIN], obj_out[k, 1, two : two + MARGIN])[0]
        last = tie(obj_out[k, 0, one : one + MARGIN], obj_out[k, 0, two : two + MARGIN])[1]
        halo_cs[0, at] = last
        halo_cs[1, at] = first
        hc_copies[at] = both(lambda i: halo_cs.at[i, at], lambda i: halo_c.at[i, at], hc_ss, hc_rs, at, left, right)

    def send_rows(k):
        hr_copies[k] = both(
            lambda i: obj_out.at[k, pl.ds(0, 2), pl.ds(MARGIN + i * (TILE - MARGIN), MARGIN)],
            lambda i: halo_r.at[i, k], hr_ss, hr_rs, k, up, down,
        )

    def take_cols(k, edge):
        one, two = (MARGIN, TILE) if edge else (2 * MARGIN, 3 * MARGIN)
        at = 2 * k + edge
        land(hc_copies[at])
        from_right = jnp.where(has_right, halo_c[0, at], 0.0)
        from_left = jnp.where(has_left, halo_c[1, at], 0.0)
        obj_out[k, 2, one : one + MARGIN] = pick(from_right, half(from_left))
        obj_out[k, 2, two : two + MARGIN] = pick(half(from_right), from_left)

    def send_corners(k):
        ho_copies[k] = both(
            lambda i: obj_out.at[k, 2, pl.ds(MARGIN + i * (TILE - MARGIN), MARGIN)],
            lambda i: corner_r.at[i, k], ho_ss, ho_rs, k, up, down,
        )

    if fold:
        fold_rows(0)
        each(N_PLANE, lambda s: rs_arrival(s).wait_recv())
        total = rs_buf[0]
        for other in range(1, N_PLANE):
            total = total + rs_buf[other]
        z_src[...] = total
        z_buf[z] = total
        each(N_Z, lambda s: z_copy(s).start())
        fold_rows(1)
        land(fm_copies)
        for k in range(2):
            update(k, (1, 2))
            if halo:
                send_cols(k, 0)
        for k in range(2):
            land(fe_copies[k])
            update(k, (0, 3))
            if halo:
                send_cols(k, 1)
                send_rows(k)
        each(N_Z, lambda s: z_arrival(s).wait_recv())
        total = z_buf[0]
        for other in range(1, N_Z):
            total = total + z_buf[other]
        probe_weight = 1.0 / (total[2] + PROBE_REG)
        for k in range(2):
            step = total[k] * probe_weight
            ag_buf[plane, k] = probe_in[core, k, plane] - step if halo else step
        each(N_PLANE, lambda s: ag_copy(s).start())
    else:
        own_spots = places_in.at[pl.ds(0, SLOTS)]
        line_copies = both(lambda i: own_spots, lambda i: line_buf.at[2 - 2 * i], spots_ss, spots_rs, 0, left, right)
        for k in range(2):
            send_cols(k, 1)
            send_rows(k)
        for k in range(2):
            send_cols(k, 0)
        line_buf[1] = places_in[:SLOTS]
        land(line_copies)
        spots_copies = both(lambda i: line_buf, lambda i: spots_buf.at[1 - i], spots_ss, spots_rs, 1, up, down)
    if halo:
        for k in range(2):
            take_cols(k, 1)
            send_corners(k)
        for k in range(2):
            take_cols(k, 0)

    if fold:
        each(N_PLANE, lambda s: ag_arrival(s).wait_recv())
        (agp,) = go(copy(ag_buf, ag_pair, agp_ss.at[0], agp_rs.at[0], pair))
        for k in range(2):
            probe_out[core, k] = ag_buf[:, k]

    if halo:
        for k in range(2):
            land(hr_copies[k])
            obj_out[k, :2, TILE + MARGIN :] = jnp.where(has_down, halo_r[0, k], 0.0)
            obj_out[k, :2, :MARGIN] = jnp.where(has_up, halo_r[1, k], 0.0)
        for k in range(2):
            land(ho_copies[k])
            obj_out[k, 2, TILE + MARGIN :] = jnp.where(has_down, corner_r[0, k], 0.0)
            obj_out[k, 2, :MARGIN] = jnp.where(has_up, corner_r[1, k], 0.0)

    if not fold:
        land(spots_copies)

        def as_row(column):
            shape = (SLOTS, W)
            diagonal = lax.broadcasted_iota(jnp.int32, shape, 0) == lax.broadcasted_iota(jnp.int32, shape, 1)
            spread_out = jnp.where(diagonal, column.astype(jnp.float32), 0.0)
            return jnp.sum(spread_out, axis=0, keepdims=True).astype(jnp.int32)

        def packed(spots):
            down_by = spots[:, :1] - (row * TILE - W)
            across = spots[:, 1:2] - (col * TILE - W)
            fits = (down_by > 0) & (down_by < TILE + W) & (across > 0) & (across < TILE + W)
            return as_row(jnp.where(fits, down_by * 1024 + across, 0))

        def count_at(far_row, far_col):
            line = places_in[pl.ds(SLOTS + jnp.clip(far_row, 0, N_ROW - 1), 1), :]
            line = jnp.where(lax.broadcasted_iota(jnp.int32, line.shape, 1) == far_col, line, 0)
            inside = jnp.logical_and(far_row >= 0, far_row < N_ROW)
            return jnp.where(inside, jnp.sum(line.astype(jnp.float32), axis=1, keepdims=True), 0.0)

        lists = [spots_buf[0, 0], spots_buf[0, 1], spots_buf[0, 2], line_buf[0], line_buf[2]]
        lists += [spots_buf[1, 0], spots_buf[1, 1], spots_buf[1, 2]]
        own_at = places_in[:SLOTS]
        slot_of = lax.broadcasted_iota(jnp.int32, (1, W), 1)
        counts = jnp.zeros((1, W), jnp.float32)
        for i, (below, across) in enumerate(NEAR + ((0, 0),)):
            counts = jnp.where(slot_of == i, count_at(row + below, col + across), counts)
        for i, one in enumerate(lists):
            spots_out[i : i + 1] = packed(one)
        spots_out[ROWS : ROWS + 1] = as_row(own_at[:, :1] - (row * TILE - MARGIN))
        spots_out[COLS : COLS + 1] = as_row(own_at[:, 1:2] - col * TILE)
        spots_out[COUNTS : COUNTS + 1] = counts.astype(jnp.int32)
        spots_out[COUNTS + 1 :] = jnp.zeros((16 - COUNTS - 1, W), jnp.int32)
    if fold:
        land([agp])
        for k in range(2):
            probe_out[1 - core, k] = ag_pair[:, k]
    for one in sent:
        one.wait_send()
    if fold:
        each(N_PLANE, lambda s: rs_copy(s).wait_send())
        each(N_Z, lambda s: z_copy(s).wait_send())
        each(N_PLANE, lambda s: ag_copy(s).wait_send())


def spread(fold, halo, number, *operands):
    vmem = pl.BlockSpec(memory_space=pltpu.VMEM)
    dma = pltpu.SemaphoreType.DMA
    f32 = jnp.float32
    outs = []
    if halo:
        outs.append(jax.ShapeDtypeStruct((2, 3, EXT, W), f32))
    if fold:
        outs.append(jax.ShapeDtypeStruct((2, TILE, TILE), f32))
    else:
        outs.append(jax.ShapeDtypeStruct((16, W), jnp.int32))
    scratch = []
    if fold:
        outs.append(jax.ShapeDtypeStruct((2, 2, 16, 8, W), f32))
        scratch += [
            pltpu.VMEM((3, 16, 8, W), f32),
            pltpu.VMEM((16, 3, 8, W), f32),
            pltpu.VMEM((16, 3, 8, W), f32),
            pltpu.VMEM((3, 8, W), f32),
            pltpu.VMEM((8, 3, 8, W), f32),
            pltpu.VMEM((16, 2, 8, W), f32),
            pltpu.VMEM((16, 2, 8, W), f32),
            pltpu.VMEM((2, 2, 3, MARGIN, W), f32),
            pltpu.VMEM((2, 3, 2 * MARGIN, W), f32),
            pltpu.VMEM((2, 2, MARGIN, W), f32),
            pltpu.VMEM((2, 2, MARGIN, W), f32),
            pltpu.VMEM((2, 2, MARGIN, W), f32),
            pltpu.VMEM((2, 2, MARGIN, W), f32),
            dma((2,)), dma((2,)), dma((16,)), dma((16,)), dma((8,)), dma((8,)), dma((16,)), dma((16,)),
            dma((1,)), dma((1,)), dma((4,)), dma((4,)), dma((2,)), dma((2,)), dma((4,)), dma((4,)),
        ]
    else:
        scratch += [
            pltpu.VMEM((3, SLOTS, N_COL), jnp.int32),
            pltpu.VMEM((2, 3, SLOTS, N_COL), jnp.int32),
            dma((4,)), dma((4,)),
        ]
    if halo:
        scratch += [
            pltpu.VMEM((2, 4, MARGIN, W), f32),
            pltpu.VMEM((2, 4, MARGIN, W), f32),
            pltpu.VMEM((2, 2, 2, MARGIN, W), f32),
            pltpu.VMEM((2, 2, MARGIN, W), f32),
            dma((8,)), dma((8,)), dma((4,)), dma((4,)), dma((4,)), dma((4,)),
        ]
    return pl.pallas_call(
        functools.partial(spread_kernel, fold, halo),
        out_shape=tuple(outs),
        in_specs=[vmem] * len(operands),
        out_specs=(vmem,) * len(outs),
        scratch_shapes=scratch,
        compiler_params=pltpu.CompilerParams(
            collective_id=number, has_side_effects=True, vmem_limit_bytes=SPREAD_VMEM
        ),
        cost_estimate=pl.CostEstimate(flops=20_000_000_000, bytes_accessed=40_000_000, transcendentals=0),
        name="spread" + str(number),
    )(*operands)


def per_device(object_slab, probe_modes, intensities, positions, live_counts):
    tables = jnp.asarray(dft_parts())
    padded = jnp.pad(positions.reshape(SLOTS, 2), ((0, 0), (0, N_COL - 2)))
    where = jnp.concatenate([padded, live_counts], axis=0)
    intens = intensities.reshape(SLOTS, W, W)
    probe = probe_modes
    current, spots = spread(False, True, 0, object_slab, where)
    for sweep in range(ITERS):
        grad, sums, weight = frames(spots, current, probe, intens, tables)
        last = sweep == ITERS - 1
        outs = spread(
            True, not last, sweep + 1,
            current, probe.reshape(2, 2, 16, 8, W), grad, sums.reshape(5, 16, 8, W), weight,
        )
        if last:
            return tile - outs[0], probe - outs[1].reshape(2, 2, W, W)
        current, tile, probe = outs
        probe = probe.reshape(2, 2, W, W)


def solution(mesh):
    return jax.shard_map(
        per_device,
        mesh=mesh,
        in_specs=(
            P(None, "row", "col"),
            P(),
            P("row", "col", None, None, None),
            P("row", "col", None, None),
            P(),
        ),
        out_specs=(P(None, "row", "col"), P()),
        check_vma=False,
    )
```

```python
import functools

import jax
import jax.numpy as jnp
import ml_dtypes
import numpy as np
from jax import lax
from jax.experimental import pallas as pl
from jax.experimental.pallas import tpu as pltpu
from jax.sharding import PartitionSpec as P

ITERS = 2
W = 128
MARGIN = 64
TILE = 256
EXT = TILE + 2 * MARGIN
SLOTS = 24
BATCH = 1
RING = 8
UNROLL = 3
ORDER = 321546
OBJECT_REG = 1.0
PROBE_REG = 1.0
FLOOR_SQ = 0.0625
TINY = 1e-36
N_ROW = 32
N_COL = 8
N_PLANE = 16
N_Z = 8
FRAMES_VMEM = 20 * 1024 * 1024
SPREAD_VMEM = 16 * 1024 * 1024
MESH = pl.DeviceIdType.MESH
NEAR = ((-1, -1), (-1, 0), (-1, 1), (0, -1), (0, 1), (1, -1), (1, 0), (1, 1))
CHUNK = 8
ROWS, COLS, COUNTS = 8, 9, 10


def dft_parts():
    counter = np.arange(W)
    angles = (counter[:, None] * counter[None, :] % W) * (2.0 * np.pi / W)
    cosine = np.cos(angles) / np.sqrt(W)
    sine = np.sin(angles) / np.sqrt(W)
    fore = np.block([[cosine, sine], [-sine, cosine]])
    back = np.block([[cosine, -sine], [sine, cosine]])

    def split(table):
        high = table.astype(np.float32).astype(ml_dtypes.bfloat16)
        low = (table - high.astype(np.float64)).astype(np.float32).astype(ml_dtypes.bfloat16)
        return high, low

    fore_hi, fore_lo = split(fore)
    back_hi, back_lo = split(back)
    return np.stack([fore_hi, fore_lo, back_hi, back_lo])


def split_two(value):
    high = value.astype(jnp.bfloat16)
    low = (value - high.astype(jnp.float32)).astype(jnp.bfloat16)
    return high, low


def dot(left, right):
    return jnp.dot(left, right, preferred_element_type=jnp.float32)


def frames_kernel(
    spots, obj, probe, intens, tables,
    grad, sums, weight, patch_buf, mid_buf, far_buf, back_buf, near_buf, light_buf, illum, listed,
):
    grad[...] = jnp.zeros_like(grad)
    sums[...] = jnp.zeros_like(sums)
    lighting = probe[0, 0] * probe[0, 0] + probe[0, 1] * probe[0, 1]
    light_buf[...] = lighting + probe[1, 0] * probe[1, 0] + probe[1, 1] * probe[1, 1]
    own = spots[COUNTS, len(NEAR)]

    def on_left(high):
        return jnp.concatenate([tables[high], tables[high + 1], tables[high]], axis=1)

    def on_right(high):
        return jnp.concatenate([tables[high], tables[high], tables[high + 1]], axis=0)

    lane = lax.broadcasted_iota(jnp.int32, (W, W), 1)

    def place(slot):
        row = spots[ROWS, slot]
        col = spots[COLS, slot]
        col = jnp.where(col < 0, col + EXT, col)
        first = lax.shift_right_logical(col, 7)
        shift = lax.bitwise_and(col, 127)
        second = jnp.where(first == 2, 0, first + 1)
        return row, first, second, shift

    def member_slot(turn, member):
        slot = turn * BATCH + member
        flag = jnp.where(jnp.logical_and(slot >= 0, slot < own), 1.0, 0.0).astype(jnp.float32)
        return jnp.clip(slot, 0, SLOTS - 1), flag

    def last_product(turn):
        halves = []
        for member in range(BATCH):
            for m in range(2):
                halves.append(jnp.concatenate([near_buf[member, m], near_buf[member, m, :, : 2 * W]], axis=1))
        return dot(jnp.concatenate(halves, axis=0), on_right(0))

    def last_adds(turn, resid):
        ring = lax.bitwise_and(turn, RING - 1)
        terms = [None] * 5
        for member in range(BATCH):
            slot, flag = member_slot(turn, member)
            row, first, second, shift = place(slot)
            keep = lane >= shift
            obj_real = patch_buf[ring, member, 0]
            obj_imag = patch_buf[ring, member, 1]
            grad_real = 0.0
            grad_imag = 0.0
            adds = []
            for m in range(2):
                base = (member * 2 + m) * W
                real = resid[base : base + W, :W]
                imag = resid[base : base + W, W:]
                grad_real = grad_real + probe[m, 0] * real + probe[m, 1] * imag
                grad_imag = grad_imag + probe[m, 0] * imag - probe[m, 1] * real
                adds.append(obj_real * real + obj_imag * imag)
                adds.append(obj_real * imag - obj_imag * real)
            adds.append((obj_real * obj_real + obj_imag * obj_imag) * flag)
            for k in range(5):
                terms[k] = adds[k] if member == 0 else terms[k] + adds[k]
            for k, piece in enumerate((grad_real, grad_imag)):
                turned = pltpu.roll(piece, shift, 1)
                grad[k, first, pl.ds(row, W), :] += jnp.where(keep, turned, 0.0)
                grad[k, second, pl.ds(row, W), :] += jnp.where(keep, 0.0, turned)
            turned = pltpu.roll(light_buf[...] * flag, shift, 1)
            at = jnp.where(first == 2, 0, first + 1)
            illum[at, pl.ds(row + MARGIN, W), :] += jnp.where(keep, turned, 0.0)
            illum[at + 1, pl.ds(row + MARGIN, W), :] += jnp.where(keep, 0.0, turned)
        for k in range(5):
            sums[k] += terms[k]

    def third_stage(turn):
        for member in range(BATCH):
            stacked = jnp.concatenate([back_buf[member, :256], back_buf[member]], axis=0)
            near = dot(on_left(2), stacked)
            real_hi, real_lo = split_two(near[:W])
            imag_hi, imag_lo = split_two(near[W:])
            for m in range(2):
                cut = slice(m * W, (m + 1) * W)
                near_buf[member, m] = jnp.concatenate(
                    [real_hi[:, cut], imag_hi[:, cut], real_lo[:, cut], imag_lo[:, cut]], axis=1
                )

    def scale(turn, far=None):
        for member in range(BATCH):
            slot, flag = member_slot(turn, member)
            far_real = far_buf[member, :W] if far is None else far[member][:W]
            far_imag = far_buf[member, W:] if far is None else far[member][W:]
            power = far_real * far_real + far_imag * far_imag
            model = jnp.maximum(power[:, :W] + power[:, W:], FLOOR_SQ)
            frame = intens[slot]
            ratio = frame * lax.rsqrt(jnp.maximum(frame * model, TINY))
            factor = (1.0 - ratio) * flag
            factor = jnp.concatenate([factor, factor], axis=1)
            real_hi, real_lo = split_two(far_real * factor)
            imag_hi, imag_lo = split_two(far_imag * factor)
            back_buf[member] = jnp.concatenate([real_hi, imag_hi, real_lo, imag_lo], axis=0)

    def second_stage(turn):
        for member in range(BATCH):
            stacked = jnp.concatenate([mid_buf[member, :256], mid_buf[member]], axis=0)
            far_buf[member] = dot(on_left(0), stacked)

    def first_stage(turn):
        ring = lax.bitwise_and(turn, RING - 1)
        rows = []
        for member in range(BATCH):
            slot, flag = member_slot(turn, member)
            row, first, second, shift = place(slot)
            back = lax.bitwise_and(128 - shift, 127)
            keep = lane >= shift
            patch = []
            for k in range(2):
                one = obj[k, first, pl.ds(row, W), :]
                two = obj[k, second, pl.ds(row, W), :]
                patch.append(pltpu.roll(jnp.where(keep, one, two), back, 1))
                patch_buf[ring, member, k] = patch[k]
            for m in range(2):
                real_hi, real_lo = split_two(probe[m, 0] * patch[0] - probe[m, 1] * patch[1])
                imag_hi, imag_lo = split_two(probe[m, 0] * patch[1] + probe[m, 1] * patch[0])
                rows.append(
                    jnp.concatenate([real_hi, imag_hi, real_lo, imag_lo, real_hi, imag_hi], axis=1)
                )
        mid = dot(jnp.concatenate(rows, axis=0), on_right(2))
        for member in range(BATCH):
            base = member * 2 * W
            real_hi, real_lo = split_two(
                jnp.concatenate([mid[base : base + W, :W], mid[base + W : base + 2 * W, :W]], axis=1)
            )
            imag_hi, imag_lo = split_two(
                jnp.concatenate([mid[base : base + W, W:], mid[base + W : base + 2 * W, W:]], axis=1)
            )
            mid_buf[member] = jnp.concatenate([real_hi, imag_hi, real_lo, imag_lo], axis=0)

    illum[...] = jnp.zeros_like(illum)
    held_count = jnp.int32(0)
    for near in range(len(NEAR)):
        there = spots[COUNTS, near]

        def gather(chunk, held):
            for k in range(CHUNK):
                slot = chunk * CHUNK + k
                packed = spots[near, slot]
                listed[held] = packed
                fits = jnp.logical_and(packed > 0, slot < there)
                held = held + jnp.where(fits, 1, 0)
            return held

        held_count = lax.fori_loop(0, (there + CHUNK - 1) // CHUNK, gather, held_count)

    def shine(step, carry):
        for k in range(2):
            entry = 2 * step + k
            live = entry < held_count
            packed = jnp.where(live, listed[jnp.where(live, entry, 0)], 1025)
            flag = jnp.where(live, 1.0, 0.0).astype(jnp.float32)
            row = lax.shift_right_logical(packed, 10)
            col = lax.bitwise_and(packed, 1023)
            first = lax.shift_right_logical(col, 7)
            shift = lax.bitwise_and(col, 127)
            keep = lane >= shift
            turned = pltpu.roll(light_buf[...] * flag, shift, 1)
            illum[first, pl.ds(row, W), :] += jnp.where(keep, turned, 0.0)
            illum[first + 1, pl.ds(row, W), :] += jnp.where(keep, 0.0, turned)
        return carry

    lax.fori_loop(0, (held_count + 1) // 2, shine, 0)

    order = str(ORDER)
    lag = {}
    for before, now in zip(" 12345", "123456"):
        lag[now] = 0 if before == " " else lag[before] + (order.index(now) < order.index(before))

    def body(turn, runs):
        held = None
        for stage in order:
            if not runs(lag[stage]):
                continue
            at = turn - lag[stage]
            if stage == "1":
                first_stage(at)
            elif stage == "2":
                second_stage(at)
            elif stage == "3":
                scale(at)
            elif stage == "4":
                third_stage(at)
            elif stage == "5":
                held = last_product(at)
            else:
                last_adds(at, held)

    depth = lag["6"]
    rounds = (jnp.maximum(own - depth, 0) + UNROLL - 1) // UNROLL

    def several(step, carry):
        for k in range(UNROLL):
            body(step * UNROLL + depth + k, lambda late: True)
        return carry

    for k in range(depth):
        body(jnp.int32(k), lambda late: late <= k)
    lax.fori_loop(0, rounds, several, 0)
    for k in range(depth):
        body(rounds * UNROLL + depth + k, lambda late: late > k)
    for part in range(2):
        weight[part] = 1.0 / (illum[part + 1, W : W + TILE, :] + OBJECT_REG)


def frames(spots, obj, probe, intens, tables):
    vmem = pl.BlockSpec(memory_space=pltpu.VMEM)
    smem = pl.BlockSpec(memory_space=pltpu.SMEM)
    return pl.pallas_call(
        frames_kernel,
        out_shape=(
            jax.ShapeDtypeStruct((2, 3, EXT, W), jnp.float32),
            jax.ShapeDtypeStruct((5, W, W), jnp.float32),
            jax.ShapeDtypeStruct((2, TILE, W), jnp.float32),
        ),
        in_specs=[smem] + [vmem] * 4,
        out_specs=(vmem, vmem, vmem),
        scratch_shapes=[
            pltpu.VMEM((RING, BATCH, 2, W, W), jnp.float32),
            pltpu.VMEM((BATCH, 4 * W, 2 * W), jnp.bfloat16),
            pltpu.VMEM((BATCH, 2 * W, 2 * W), jnp.float32),
            pltpu.VMEM((BATCH, 4 * W, 2 * W), jnp.bfloat16),
            pltpu.VMEM((BATCH, 2, W, 4 * W), jnp.bfloat16),
            pltpu.VMEM((W, W), jnp.float32),
            pltpu.VMEM((4, 2 * TILE, W), jnp.float32),
            pltpu.SMEM((len(NEAR) * SLOTS + CHUNK,), jnp.int32),
        ],
        compiler_params=pltpu.CompilerParams(vmem_limit_bytes=FRAMES_VMEM),
        cost_estimate=pl.CostEstimate(flops=9_600_000_000, bytes_accessed=10_000_000, transcendentals=0),
        name="frames",
    )(spots, obj, probe, intens, tables)


def own_place():
    row = lax.axis_index("row")
    col = lax.axis_index("col")
    core = row % 2
    z_hi = (row // 2) % 4
    x = row // 8
    y = col // 2
    z_lo = col % 2
    return row, col, core, x, y, z_hi, z_lo


def spread_kernel(fold, halo, *refs):
    refs = list(refs)
    take = lambda n: [refs.pop(0) for _ in range(n)]
    if fold:
        obj_in, probe_in, grad, sums, weight_in = take(5)
    else:
        obj_in, places_in = take(2)
    (obj_out,) = take(1)
    if not fold:
        (spots_out,) = take(1)
        line_buf, spots_buf, spots_ss, spots_rs = take(4)
    if fold:
        if halo:
            (tile_out,) = take(1)
        (probe_out,) = take(1)
        (pair_buf, rs_src, rs_buf, z_src, z_buf, ag_buf, ag_pair, fold_r, mid, mid_s, mid_r, edge_s, edge_r) = take(13)
        (pair_ss, pair_rs, rs_ss, rs_rs, z_ss, z_rs, ag_ss, ag_rs, agp_ss, agp_rs) = take(10)
        (fr_ss, fr_rs, fm_ss, fm_rs, fe_ss, fe_rs) = take(6)
    if halo:
        halo_cs, halo_c, halo_r, corner_r, hc_ss, hc_rs, hr_ss, hr_rs, ho_ss, ho_rs = take(10)

    row, col, core, x, y, z_hi, z_lo = own_place()
    plane = x * 4 + y
    z = z_hi * 2 + z_lo
    up = (lax.rem(row + N_ROW - 1, N_ROW), col)
    down = (lax.rem(row + 1, N_ROW), col)
    left = (row, lax.rem(col + N_COL - 1, N_COL))
    right = (row, lax.rem(col + 1, N_COL))
    pair = (row + 1 - 2 * core, col)
    has_up = row > 0
    has_down = row < N_ROW - 1
    has_left = col > 0
    has_right = col < N_COL - 1

    def turn(value, size):
        return jnp.where(value >= size, value - size, value)

    def plane_mate(step):
        far_x = turn(x + step // 4, 4)
        far_y = turn(y + step % 4, 4)
        return far_x * 4 + far_y, ((far_x * 4 + z_hi) * 2 + core, far_y * 2 + z_lo)

    def plane_source(step):
        return turn(x + (4 - step // 4) % 4, 4) * 4 + turn(y + (4 - step % 4) % 4, 4)

    def z_mate(step):
        other = turn(z + step, N_Z)
        return other, ((x * 4 + other // 2) * 2 + core, y * 2 + other % 2)

    def copy(src, dst, ss, rs, device):
        return pltpu.make_async_remote_copy(
            src_ref=src, dst_ref=dst, send_sem=ss, recv_sem=rs, device_id=device, device_id_type=MESH
        )

    barrier = pltpu.get_barrier_semaphore()

    def greet(device):
        pl.semaphore_signal(barrier, inc=1, device_id=device, device_id_type=MESH)

    for device in (up, down, left, right):
        greet(device)
    greeted = 4
    if fold:
        greet(pair)
        for step in range(1, N_PLANE):
            greet(plane_mate(step)[1])
        for step in range(1, N_Z):
            greet(z_mate(step)[1])
        greeted += 1 + N_PLANE - 1 + N_Z - 1
    pl.semaphore_wait(barrier, greeted)

    def pick(first, second):
        shape = jnp.shape(first) or jnp.shape(second)
        return jnp.where(lax.broadcasted_iota(jnp.int32, shape, 1) < MARGIN, first, second)

    def half(value):
        return pltpu.roll(value, MARGIN, 1)

    def rs_copy(step):
        other, device = plane_mate(step)
        return copy(rs_src.at[other], rs_buf.at[plane], rs_ss.at[step], rs_rs.at[step], device)

    def rs_arrival(step):
        other = plane_source(step)
        return copy(rs_src.at[other], rs_buf.at[other], rs_ss.at[step], rs_rs.at[step], up)

    def z_copy(step):
        return copy(z_src, z_buf.at[z], z_ss.at[step], z_rs.at[step], z_mate(step)[1])

    def z_arrival(step):
        other = turn(z + N_Z - step, N_Z)
        return copy(z_src, z_buf.at[other], z_ss.at[step], z_rs.at[step], up)

    def ag_copy(step):
        return copy(ag_buf.at[plane], ag_buf.at[plane], ag_ss.at[step], ag_rs.at[step], plane_mate(step)[1])

    def ag_arrival(step):
        other = plane_source(step)
        return copy(ag_buf.at[other], ag_buf.at[other], ag_ss.at[step], ag_rs.at[step], up)

    def each(count, act):
        for step in range(1, count):
            act(step)

    sent = []

    def go(*copies):
        for one in copies:
            one.start()
            sent.append(one)
        return copies

    def land(copies):
        for one in copies:
            one.wait_recv()

    def both(src, dst, ss, rs, at, first, second):
        return go(
            copy(src(0), dst(0), ss.at[2 * at], rs.at[2 * at], first),
            copy(src(1), dst(1), ss.at[2 * at + 1], rs.at[2 * at + 1], second),
        )

    def tie(upper, lower):
        return pick(half(upper), lower), pick(upper, half(lower))

    if fold:
        pair_copies = go(
            copy(sums.at[pl.ds(2 * (1 - core), 2)], pair_buf.at[pl.ds(0, 2)], pair_ss.at[0], pair_rs.at[0], pair),
            copy(sums.at[pl.ds(4, 1)], pair_buf.at[pl.ds(2, 1)], pair_ss.at[1], pair_rs.at[1], pair),
        )
        fr_copies = {}
        for k in range(2):
            fr_copies[k] = both(
                lambda i: grad.at[k, :, pl.ds(i * (TILE + MARGIN), MARGIN)],
                lambda i: fold_r.at[i, k], fr_ss, fr_rs, k, up, down,
            )
        for k in range(2):
            packs = tie(grad[k, 2, 2 * MARGIN : 3 * MARGIN], grad[k, 2, 3 * MARGIN : 4 * MARGIN])
            for i in range(2):
                mid_s[i, k] = packs[i]
        fm_copies = both(lambda i: mid_s.at[i], lambda i: mid_r.at[i], fm_ss, fm_rs, 0, left, right)

        land(pair_copies)
        for k in range(3):
            own = sums[4] if k == 2 else sums[2 * core + k]
            rs_src[:, k] = own + pair_buf[k]
        each(N_PLANE, lambda s: rs_copy(s).start())
        rs_buf[plane] = rs_src[plane]

        fe_copies = {}

        def fold_rows(k):
            land(fr_copies[k])
            mid[k, :, :MARGIN] = grad[k, :, MARGIN : 2 * MARGIN] + jnp.where(has_up, fold_r[1, k], 0.0)
            mid[k, :, MARGIN:] = grad[k, :, TILE : TILE + MARGIN] + jnp.where(has_down, fold_r[0, k], 0.0)
            packs = tie(mid[k, 2, :MARGIN], mid[k, 2, MARGIN:])
            for i in range(2):
                edge_s[i, k] = packs[i]
            fe_copies[k] = both(
                lambda i: edge_s.at[i, k], lambda i: edge_r.at[i, k], fe_ss, fe_rs, k, left, right
            )

        def block_of(k, block):
            if block in (0, 3):
                start = 0 if block == 0 else MARGIN
                base = [mid[k, part, start : start + MARGIN] for part in range(2)]
                got = edge_r
            else:
                start = MARGIN + block * MARGIN
                base = [grad[k, part, start : start + MARGIN] for part in range(2)]
                got = mid_r
            from_right = jnp.where(has_right, got[0, k], 0.0)
            from_left = jnp.where(has_left, got[1, k], 0.0)
            if block in (0, 1):
                from_right = half(from_right)
            else:
                from_left = half(from_left)
            return base[0] + pick(from_left, 0.0), base[1] + pick(0.0, from_right)

        def update(k, blocks):
            for block in blocks:
                parts = block_of(k, block)
                start = block * MARGIN
                for part in range(2):
                    step = parts[part] * weight_in[part, start : start + MARGIN]
                    cut = slice(part * W, (part + 1) * W)
                    if halo:
                        new = obj_in[k, part, MARGIN + start : 2 * MARGIN + start] - step
                        obj_out[k, part, MARGIN + start : 2 * MARGIN + start] = new
                        tile_out[k, start : start + MARGIN, cut] = new
                    else:
                        obj_out[k, start : start + MARGIN, cut] = step
    else:
        for k in range(2):
            for part in range(2):
                obj_out[k, part, MARGIN : MARGIN + TILE] = obj_in[k, :, part * W : (part + 1) * W]

    hc_copies = {}
    hr_copies = {}
    ho_copies = {}

    def send_cols(k, edge):
        one, two = (MARGIN, TILE) if edge else (2 * MARGIN, 3 * MARGIN)
        at = 2 * k + edge
        first = tie(obj_out[k, 1, one : one + MARGIN], obj_out[k, 1, two : two + MARGIN])[0]
        last = tie(obj_out[k, 0, one : one + MARGIN], obj_out[k, 0, two : two + MARGIN])[1]
        halo_cs[0, at] = last
        halo_cs[1, at] = first
        hc_copies[at] = both(lambda i: halo_cs.at[i, at], lambda i: halo_c.at[i, at], hc_ss, hc_rs, at, left, right)

    def send_rows(k):
        hr_copies[k] = both(
            lambda i: obj_out.at[k, pl.ds(0, 2), pl.ds(MARGIN + i * (TILE - MARGIN), MARGIN)],
            lambda i: halo_r.at[i, k], hr_ss, hr_rs, k, up, down,
        )

    def take_cols(k, edge):
        one, two = (MARGIN, TILE) if edge else (2 * MARGIN, 3 * MARGIN)
        at = 2 * k + edge
        land(hc_copies[at])
        from_right = jnp.where(has_right, halo_c[0, at], 0.0)
        from_left = jnp.where(has_left, halo_c[1, at], 0.0)
        obj_out[k, 2, one : one + MARGIN] = pick(from_right, half(from_left))
        obj_out[k, 2, two : two + MARGIN] = pick(half(from_right), from_left)

    def send_corners(k):
        ho_copies[k] = both(
            lambda i: obj_out.at[k, 2, pl.ds(MARGIN + i * (TILE - MARGIN), MARGIN)],
            lambda i: corner_r.at[i, k], ho_ss, ho_rs, k, up, down,
        )

    if fold:
        fold_rows(0)
        each(N_PLANE, lambda s: rs_arrival(s).wait_recv())
        total = rs_buf[0]
        for other in range(1, N_PLANE):
            total = total + rs_buf[other]
        z_src[...] = total
        z_buf[z] = total
        each(N_Z, lambda s: z_copy(s).start())
        fold_rows(1)
        land(fm_copies)
        for k in range(2):
            update(k, (1, 2))
            if halo:
                send_cols(k, 0)
        for k in range(2):
            land(fe_copies[k])
            update(k, (0, 3))
            if halo:
                send_cols(k, 1)
                send_rows(k)
        each(N_Z, lambda s: z_arrival(s).wait_recv())
        total = z_buf[0]
        for other in range(1, N_Z):
            total = total + z_buf[other]
        probe_weight = 1.0 / (total[2] + PROBE_REG)
        for k in range(2):
            step = total[k] * probe_weight
            ag_buf[plane, k] = probe_in[core, k, plane] - step if halo else step
        each(N_PLANE, lambda s: ag_copy(s).start())
    else:
        own_spots = places_in.at[pl.ds(0, SLOTS)]
        line_copies = both(lambda i: own_spots, lambda i: line_buf.at[2 - 2 * i], spots_ss, spots_rs, 0, left, right)
        for k in range(2):
            send_cols(k, 1)
            send_rows(k)
        for k in range(2):
            send_cols(k, 0)
        line_buf[1] = places_in[:SLOTS]
        land(line_copies)
        spots_copies = both(lambda i: line_buf, lambda i: spots_buf.at[1 - i], spots_ss, spots_rs, 1, up, down)
    if halo:
        for k in range(2):
            take_cols(k, 1)
            send_corners(k)
        for k in range(2):
            take_cols(k, 0)

    if fold:
        each(N_PLANE, lambda s: ag_arrival(s).wait_recv())
        (agp,) = go(copy(ag_buf, ag_pair, agp_ss.at[0], agp_rs.at[0], pair))
        for k in range(2):
            probe_out[core, k] = ag_buf[:, k]

    if halo:
        for k in range(2):
            land(hr_copies[k])
            obj_out[k, :2, TILE + MARGIN :] = jnp.where(has_down, halo_r[0, k], 0.0)
            obj_out[k, :2, :MARGIN] = jnp.where(has_up, halo_r[1, k], 0.0)
        for k in range(2):
            land(ho_copies[k])
            obj_out[k, 2, TILE + MARGIN :] = jnp.where(has_down, corner_r[0, k], 0.0)
            obj_out[k, 2, :MARGIN] = jnp.where(has_up, corner_r[1, k], 0.0)

    if not fold:
        land(spots_copies)

        def as_row(column):
            shape = (SLOTS, W)
            diagonal = lax.broadcasted_iota(jnp.int32, shape, 0) == lax.broadcasted_iota(jnp.int32, shape, 1)
            spread_out = jnp.where(diagonal, column.astype(jnp.float32), 0.0)
            return jnp.sum(spread_out, axis=0, keepdims=True).astype(jnp.int32)

        def packed(spots):
            down_by = spots[:, :1] - (row * TILE - W)
            across = spots[:, 1:2] - (col * TILE - W)
            fits = (down_by > 0) & (down_by < TILE + W) & (across > 0) & (across < TILE + W)
            return as_row(jnp.where(fits, down_by * 1024 + across, 0))

        def count_at(far_row, far_col):
            line = places_in[pl.ds(SLOTS + jnp.clip(far_row, 0, N_ROW - 1), 1), :]
            line = jnp.where(lax.broadcasted_iota(jnp.int32, line.shape, 1) == far_col, line, 0)
            inside = jnp.logical_and(far_row >= 0, far_row < N_ROW)
            return jnp.where(inside, jnp.sum(line.astype(jnp.float32), axis=1, keepdims=True), 0.0)

        lists = [spots_buf[0, 0], spots_buf[0, 1], spots_buf[0, 2], line_buf[0], line_buf[2]]
        lists += [spots_buf[1, 0], spots_buf[1, 1], spots_buf[1, 2]]
        own_at = places_in[:SLOTS]
        slot_of = lax.broadcasted_iota(jnp.int32, (1, W), 1)
        counts = jnp.zeros((1, W), jnp.float32)
        for i, (below, across) in enumerate(NEAR + ((0, 0),)):
            counts = jnp.where(slot_of == i, count_at(row + below, col + across), counts)
        for i, one in enumerate(lists):
            spots_out[i : i + 1] = packed(one)
        spots_out[ROWS : ROWS + 1] = as_row(own_at[:, :1] - (row * TILE - MARGIN))
        spots_out[COLS : COLS + 1] = as_row(own_at[:, 1:2] - col * TILE)
        spots_out[COUNTS : COUNTS + 1] = counts.astype(jnp.int32)
        spots_out[COUNTS + 1 :] = jnp.zeros((16 - COUNTS - 1, W), jnp.int32)
    if fold:
        land([agp])
        for k in range(2):
            probe_out[1 - core, k] = ag_pair[:, k]
    for one in sent:
        one.wait_send()
    if fold:
        each(N_PLANE, lambda s: rs_copy(s).wait_send())
        each(N_Z, lambda s: z_copy(s).wait_send())
        each(N_PLANE, lambda s: ag_copy(s).wait_send())


def spread(fold, halo, number, *operands):
    vmem = pl.BlockSpec(memory_space=pltpu.VMEM)
    dma = pltpu.SemaphoreType.DMA
    f32 = jnp.float32
    outs = []
    if halo:
        outs.append(jax.ShapeDtypeStruct((2, 3, EXT, W), f32))
    if fold:
        outs.append(jax.ShapeDtypeStruct((2, TILE, TILE), f32))
    else:
        outs.append(jax.ShapeDtypeStruct((16, W), jnp.int32))
    scratch = []
    if fold:
        outs.append(jax.ShapeDtypeStruct((2, 2, 16, 8, W), f32))
        scratch += [
            pltpu.VMEM((3, 16, 8, W), f32),
            pltpu.VMEM((16, 3, 8, W), f32),
            pltpu.VMEM((16, 3, 8, W), f32),
            pltpu.VMEM((3, 8, W), f32),
            pltpu.VMEM((8, 3, 8, W), f32),
            pltpu.VMEM((16, 2, 8, W), f32),
            pltpu.VMEM((16, 2, 8, W), f32),
            pltpu.VMEM((2, 2, 3, MARGIN, W), f32),
            pltpu.VMEM((2, 3, 2 * MARGIN, W), f32),
            pltpu.VMEM((2, 2, MARGIN, W), f32),
            pltpu.VMEM((2, 2, MARGIN, W), f32),
            pltpu.VMEM((2, 2, MARGIN, W), f32),
            pltpu.VMEM((2, 2, MARGIN, W), f32),
            dma((2,)), dma((2,)), dma((16,)), dma((16,)), dma((8,)), dma((8,)), dma((16,)), dma((16,)),
            dma((1,)), dma((1,)), dma((4,)), dma((4,)), dma((2,)), dma((2,)), dma((4,)), dma((4,)),
        ]
    else:
        scratch += [
            pltpu.VMEM((3, SLOTS, N_COL), jnp.int32),
            pltpu.VMEM((2, 3, SLOTS, N_COL), jnp.int32),
            dma((4,)), dma((4,)),
        ]
    if halo:
        scratch += [
            pltpu.VMEM((2, 4, MARGIN, W), f32),
            pltpu.VMEM((2, 4, MARGIN, W), f32),
            pltpu.VMEM((2, 2, 2, MARGIN, W), f32),
            pltpu.VMEM((2, 2, MARGIN, W), f32),
            dma((8,)), dma((8,)), dma((4,)), dma((4,)), dma((4,)), dma((4,)),
        ]
    return pl.pallas_call(
        functools.partial(spread_kernel, fold, halo),
        out_shape=tuple(outs),
        in_specs=[vmem] * len(operands),
        out_specs=(vmem,) * len(outs),
        scratch_shapes=scratch,
        compiler_params=pltpu.CompilerParams(
            collective_id=number, has_side_effects=True, vmem_limit_bytes=SPREAD_VMEM
        ),
        cost_estimate=pl.CostEstimate(flops=20_000_000_000, bytes_accessed=40_000_000, transcendentals=0),
        name="spread" + str(number),
    )(*operands)


def per_device(object_slab, probe_modes, intensities, positions, live_counts):
    tables = jnp.asarray(dft_parts())
    padded = jnp.pad(positions.reshape(SLOTS, 2), ((0, 0), (0, N_COL - 2)))
    where = jnp.concatenate([padded, live_counts], axis=0)
    intens = intensities.reshape(SLOTS, W, W)
    probe = probe_modes
    current, spots = spread(False, True, 0, object_slab, where)
    for sweep in range(ITERS):
        grad, sums, weight = frames(spots, current, probe, intens, tables)
        last = sweep == ITERS - 1
        outs = spread(
            True, not last, sweep + 1,
            current, probe.reshape(2, 2, 16, 8, W), grad, sums.reshape(5, 16, 8, W), weight,
        )
        if last:
            return tile - outs[0], probe - outs[1].reshape(2, 2, W, W)
        current, tile, probe = outs
        probe = probe.reshape(2, 2, W, W)


def solution(mesh):
    return jax.shard_map(
        per_device,
        mesh=mesh,
        in_specs=(
            P(None, "row", "col"),
            P(),
            P("row", "col", None, None, None),
            P("row", "col", None, None),
            P(),
        ),
        out_specs=(P(None, "row", "col"), P()),
        check_vma=False,
    )
```

```python
import functools

import jax
import jax.numpy as jnp
import ml_dtypes
import numpy as np
from jax import lax
from jax.experimental import pallas as pl
from jax.experimental.pallas import tpu as pltpu
from jax.sharding import PartitionSpec as P

ITERS = 2
W = 128
MARGIN = 64
TILE = 256
EXT = TILE + 2 * MARGIN
SLOTS = 24
BATCH = 1
RING = 8
UNROLL = 3
ORDER = 321546
OBJECT_REG = 1.0
PROBE_REG = 1.0
FLOOR_SQ = 0.0625
TINY = 1e-36
N_ROW = 32
N_COL = 8
N_PLANE = 16
N_Z = 8
FRAMES_VMEM = 20 * 1024 * 1024
SPREAD_VMEM = 16 * 1024 * 1024
MESH = pl.DeviceIdType.MESH
NEAR = ((-1, -1), (-1, 0), (-1, 1), (0, -1), (0, 1), (1, -1), (1, 0), (1, 1))
CHUNK = 8
ROWS, COLS, COUNTS = 8, 9, 10


def dft_parts():
    counter = np.arange(W)
    angles = (counter[:, None] * counter[None, :] % W) * (2.0 * np.pi / W)
    cosine = np.cos(angles) / np.sqrt(W)
    sine = np.sin(angles) / np.sqrt(W)
    fore = np.block([[cosine, sine], [-sine, cosine]])
    back = np.block([[cosine, -sine], [sine, cosine]])

    def split(table):
        high = table.astype(np.float32).astype(ml_dtypes.bfloat16)
        low = (table - high.astype(np.float64)).astype(np.float32).astype(ml_dtypes.bfloat16)
        return high, low

    fore_hi, fore_lo = split(fore)
    back_hi, back_lo = split(back)
    return np.stack([fore_hi, fore_lo, back_hi, back_lo])


def split_two(value):
    high = value.astype(jnp.bfloat16)
    low = (value - high.astype(jnp.float32)).astype(jnp.bfloat16)
    return high, low


def dot(left, right):
    return jnp.dot(left, right, preferred_element_type=jnp.float32)


def frames_kernel(
    spots, obj, probe, intens, tables,
    grad, sums, weight, patch_buf, mid_buf, far_buf, back_buf, near_buf, light_buf, illum, listed,
):
    grad[...] = jnp.zeros_like(grad)
    sums[...] = jnp.zeros_like(sums)
    lighting = probe[0, 0] * probe[0, 0] + probe[0, 1] * probe[0, 1]
    light_buf[...] = lighting + probe[1, 0] * probe[1, 0] + probe[1, 1] * probe[1, 1]
    own = spots[len(NEAR), COUNTS]

    def on_left(high):
        return jnp.concatenate([tables[high], tables[high + 1], tables[high]], axis=1)

    def on_right(high):
        return jnp.concatenate([tables[high], tables[high], tables[high + 1]], axis=0)

    lane = lax.broadcasted_iota(jnp.int32, (W, W), 1)

    def place(slot):
        row = spots[slot, ROWS]
        col = spots[slot, COLS]
        col = jnp.where(col < 0, col + EXT, col)
        first = lax.shift_right_logical(col, 7)
        shift = lax.bitwise_and(col, 127)
        second = jnp.where(first == 2, 0, first + 1)
        return row, first, second, shift

    def member_slot(turn, member):
        slot = turn * BATCH + member
        flag = jnp.where(jnp.logical_and(slot >= 0, slot < own), 1.0, 0.0).astype(jnp.float32)
        return jnp.clip(slot, 0, SLOTS - 1), flag

    def last_product(turn):
        halves = []
        for member in range(BATCH):
            for m in range(2):
                halves.append(jnp.concatenate([near_buf[member, m], near_buf[member, m, :, : 2 * W]], axis=1))
        return dot(jnp.concatenate(halves, axis=0), on_right(0))

    def last_adds(turn, resid):
        ring = lax.bitwise_and(turn, RING - 1)
        terms = [None] * 5
        for member in range(BATCH):
            slot, flag = member_slot(turn, member)
            row, first, second, shift = place(slot)
            keep = lane >= shift
            obj_real = patch_buf[ring, member, 0]
            obj_imag = patch_buf[ring, member, 1]
            grad_real = 0.0
            grad_imag = 0.0
            adds = []
            for m in range(2):
                base = (member * 2 + m) * W
                real = resid[base : base + W, :W]
                imag = resid[base : base + W, W:]
                grad_real = grad_real + probe[m, 0] * real + probe[m, 1] * imag
                grad_imag = grad_imag + probe[m, 0] * imag - probe[m, 1] * real
                adds.append(obj_real * real + obj_imag * imag)
                adds.append(obj_real * imag - obj_imag * real)
            adds.append((obj_real * obj_real + obj_imag * obj_imag) * flag)
            for k in range(5):
                terms[k] = adds[k] if member == 0 else terms[k] + adds[k]
            for k, piece in enumerate((grad_real, grad_imag)):
                turned = pltpu.roll(piece, shift, 1)
                grad[k, first, pl.ds(row, W), :] += jnp.where(keep, turned, 0.0)
                grad[k, second, pl.ds(row, W), :] += jnp.where(keep, 0.0, turned)
            turned = pltpu.roll(light_buf[...] * flag, shift, 1)
            at = jnp.where(first == 2, 0, first + 1)
            illum[at, pl.ds(row + MARGIN, W), :] += jnp.where(keep, turned, 0.0)
            illum[at + 1, pl.ds(row + MARGIN, W), :] += jnp.where(keep, 0.0, turned)
        for k in range(5):
            sums[k] += terms[k]

    def third_stage(turn):
        for member in range(BATCH):
            stacked = jnp.concatenate([back_buf[member, :256], back_buf[member]], axis=0)
            near = dot(on_left(2), stacked)
            real_hi, real_lo = split_two(near[:W])
            imag_hi, imag_lo = split_two(near[W:])
            for m in range(2):
                cut = slice(m * W, (m + 1) * W)
                near_buf[member, m] = jnp.concatenate(
                    [real_hi[:, cut], imag_hi[:, cut], real_lo[:, cut], imag_lo[:, cut]], axis=1
                )

    def scale(turn, far=None):
        for member in range(BATCH):
            slot, flag = member_slot(turn, member)
            far_real = far_buf[member, :W] if far is None else far[member][:W]
            far_imag = far_buf[member, W:] if far is None else far[member][W:]
            power = far_real * far_real + far_imag * far_imag
            model = jnp.maximum(power[:, :W] + power[:, W:], FLOOR_SQ)
            frame = intens[slot]
            ratio = frame * lax.rsqrt(jnp.maximum(frame * model, TINY))
            factor = (1.0 - ratio) * flag
            factor = jnp.concatenate([factor, factor], axis=1)
            real_hi, real_lo = split_two(far_real * factor)
            imag_hi, imag_lo = split_two(far_imag * factor)
            back_buf[member] = jnp.concatenate([real_hi, imag_hi, real_lo, imag_lo], axis=0)

    def second_stage(turn):
        for member in range(BATCH):
            stacked = jnp.concatenate([mid_buf[member, :256], mid_buf[member]], axis=0)
            far_buf[member] = dot(on_left(0), stacked)

    def first_stage(turn):
        ring = lax.bitwise_and(turn, RING - 1)
        rows = []
        for member in range(BATCH):
            slot, flag = member_slot(turn, member)
            row, first, second, shift = place(slot)
            back = lax.bitwise_and(128 - shift, 127)
            keep = lane >= shift
            patch = []
            for k in range(2):
                one = obj[k, first, pl.ds(row, W), :]
                two = obj[k, second, pl.ds(row, W), :]
                patch.append(pltpu.roll(jnp.where(keep, one, two), back, 1))
                patch_buf[ring, member, k] = patch[k]
            for m in range(2):
                real_hi, real_lo = split_two(probe[m, 0] * patch[0] - probe[m, 1] * patch[1])
                imag_hi, imag_lo = split_two(probe[m, 0] * patch[1] + probe[m, 1] * patch[0])
                rows.append(
                    jnp.concatenate([real_hi, imag_hi, real_lo, imag_lo, real_hi, imag_hi], axis=1)
                )
        mid = dot(jnp.concatenate(rows, axis=0), on_right(2))
        for member in range(BATCH):
            base = member * 2 * W
            real_hi, real_lo = split_two(
                jnp.concatenate([mid[base : base + W, :W], mid[base + W : base + 2 * W, :W]], axis=1)
            )
            imag_hi, imag_lo = split_two(
                jnp.concatenate([mid[base : base + W, W:], mid[base + W : base + 2 * W, W:]], axis=1)
            )
            mid_buf[member] = jnp.concatenate([real_hi, imag_hi, real_lo, imag_lo], axis=0)

    illum[...] = jnp.zeros_like(illum)
    held_count = jnp.int32(0)
    for near in range(len(NEAR)):
        there = spots[near, COUNTS]

        def gather(chunk, held):
            for k in range(CHUNK):
                slot = chunk * CHUNK + k
                packed = spots[slot, near]
                listed[held] = packed
                fits = jnp.logical_and(packed > 0, slot < there)
                held = held + jnp.where(fits, 1, 0)
            return held

        held_count = lax.fori_loop(0, (there + CHUNK - 1) // CHUNK, gather, held_count)

    def shine(step, carry):
        for k in range(2):
            entry = 2 * step + k
            live = entry < held_count
            packed = jnp.where(live, listed[jnp.where(live, entry, 0)], 1025)
            flag = jnp.where(live, 1.0, 0.0).astype(jnp.float32)
            row = lax.shift_right_logical(packed, 10)
            col = lax.bitwise_and(packed, 1023)
            first = lax.shift_right_logical(col, 7)
            shift = lax.bitwise_and(col, 127)
            keep = lane >= shift
            turned = pltpu.roll(light_buf[...] * flag, shift, 1)
            illum[first, pl.ds(row, W), :] += jnp.where(keep, turned, 0.0)
            illum[first + 1, pl.ds(row, W), :] += jnp.where(keep, 0.0, turned)
        return carry

    lax.fori_loop(0, (held_count + 1) // 2, shine, 0)

    order = str(ORDER)
    lag = {}
    for before, now in zip(" 12345", "123456"):
        lag[now] = 0 if before == " " else lag[before] + (order.index(now) < order.index(before))

    def body(turn, runs):
        held = None
        for stage in order:
            if not runs(lag[stage]):
                continue
            at = turn - lag[stage]
            if stage == "1":
                first_stage(at)
            elif stage == "2":
                second_stage(at)
            elif stage == "3":
                scale(at)
            elif stage == "4":
                third_stage(at)
            elif stage == "5":
                held = last_product(at)
            else:
                last_adds(at, held)

    depth = lag["6"]
    rounds = (jnp.maximum(own - depth, 0) + UNROLL - 1) // UNROLL

    def several(step, carry):
        for k in range(UNROLL):
            body(step * UNROLL + depth + k, lambda late: True)
        return carry

    for k in range(depth):
        body(jnp.int32(k), lambda late: late <= k)
    lax.fori_loop(0, rounds, several, 0)
    for k in range(depth):
        body(rounds * UNROLL + depth + k, lambda late: late > k)
    for part in range(2):
        weight[part] = 1.0 / (illum[part + 1, W : W + TILE, :] + OBJECT_REG)


def frames(spots, obj, probe, intens, tables):
    vmem = pl.BlockSpec(memory_space=pltpu.VMEM)
    smem = pl.BlockSpec(memory_space=pltpu.SMEM)
    return pl.pallas_call(
        frames_kernel,
        out_shape=(
            jax.ShapeDtypeStruct((2, 3, EXT, W), jnp.float32),
            jax.ShapeDtypeStruct((5, W, W), jnp.float32),
            jax.ShapeDtypeStruct((2, TILE, W), jnp.float32),
        ),
        in_specs=[smem] + [vmem] * 4,
        out_specs=(vmem, vmem, vmem),
        scratch_shapes=[
            pltpu.VMEM((RING, BATCH, 2, W, W), jnp.float32),
            pltpu.VMEM((BATCH, 4 * W, 2 * W), jnp.bfloat16),
            pltpu.VMEM((BATCH, 2 * W, 2 * W), jnp.float32),
            pltpu.VMEM((BATCH, 4 * W, 2 * W), jnp.bfloat16),
            pltpu.VMEM((BATCH, 2, W, 4 * W), jnp.bfloat16),
            pltpu.VMEM((W, W), jnp.float32),
            pltpu.VMEM((4, 2 * TILE, W), jnp.float32),
            pltpu.SMEM((len(NEAR) * SLOTS + CHUNK,), jnp.int32),
        ],
        compiler_params=pltpu.CompilerParams(vmem_limit_bytes=FRAMES_VMEM),
        cost_estimate=pl.CostEstimate(flops=9_600_000_000, bytes_accessed=10_000_000, transcendentals=0),
        name="frames",
    )(spots, obj, probe, intens, tables)


def own_place():
    row = lax.axis_index("row")
    col = lax.axis_index("col")
    core = row % 2
    z_hi = (row // 2) % 4
    x = row // 8
    y = col // 2
    z_lo = col % 2
    return row, col, core, x, y, z_hi, z_lo


def spread_kernel(fold, halo, *refs):
    refs = list(refs)
    take = lambda n: [refs.pop(0) for _ in range(n)]
    if fold:
        obj_in, probe_in, grad, sums, weight_in = take(5)
    else:
        obj_in, places_in = take(2)
    (obj_out,) = take(1)
    if not fold:
        (spots_out,) = take(1)
        line_buf, spots_buf, spots_ss, spots_rs = take(4)
    if fold:
        if halo:
            (tile_out,) = take(1)
        (probe_out,) = take(1)
        (pair_buf, rs_src, rs_buf, z_src, z_buf, ag_buf, ag_pair, fold_r, mid, mid_s, mid_r, edge_s, edge_r) = take(13)
        (pair_ss, pair_rs, rs_ss, rs_rs, z_ss, z_rs, ag_ss, ag_rs, agp_ss, agp_rs) = take(10)
        (fr_ss, fr_rs, fm_ss, fm_rs, fe_ss, fe_rs) = take(6)
    if halo:
        halo_cs, halo_c, halo_r, corner_r, hc_ss, hc_rs, hr_ss, hr_rs, ho_ss, ho_rs = take(10)

    row, col, core, x, y, z_hi, z_lo = own_place()
    plane = x * 4 + y
    z = z_hi * 2 + z_lo
    up = (lax.rem(row + N_ROW - 1, N_ROW), col)
    down = (lax.rem(row + 1, N_ROW), col)
    left = (row, lax.rem(col + N_COL - 1, N_COL))
    right = (row, lax.rem(col + 1, N_COL))
    pair = (row + 1 - 2 * core, col)
    has_up = row > 0
    has_down = row < N_ROW - 1
    has_left = col > 0
    has_right = col < N_COL - 1

    def turn(value, size):
        return jnp.where(value >= size, value - size, value)

    def plane_mate(step):
        far_x = turn(x + step // 4, 4)
        far_y = turn(y + step % 4, 4)
        return far_x * 4 + far_y, ((far_x * 4 + z_hi) * 2 + core, far_y * 2 + z_lo)

    def plane_source(step):
        return turn(x + (4 - step // 4) % 4, 4) * 4 + turn(y + (4 - step % 4) % 4, 4)

    def z_mate(step):
        other = turn(z + step, N_Z)
        return other, ((x * 4 + other // 2) * 2 + core, y * 2 + other % 2)

    def copy(src, dst, ss, rs, device):
        return pltpu.make_async_remote_copy(
            src_ref=src, dst_ref=dst, send_sem=ss, recv_sem=rs, device_id=device, device_id_type=MESH
        )

    barrier = pltpu.get_barrier_semaphore()

    def greet(device):
        pl.semaphore_signal(barrier, inc=1, device_id=device, device_id_type=MESH)

    for device in (up, down, left, right):
        greet(device)
    greeted = 4
    if fold:
        greet(pair)
        for step in range(1, N_PLANE):
            greet(plane_mate(step)[1])
        for step in range(1, N_Z):
            greet(z_mate(step)[1])
        greeted += 1 + N_PLANE - 1 + N_Z - 1
    pl.semaphore_wait(barrier, greeted)

    def pick(first, second):
        shape = jnp.shape(first) or jnp.shape(second)
        return jnp.where(lax.broadcasted_iota(jnp.int32, shape, 1) < MARGIN, first, second)

    def half(value):
        return pltpu.roll(value, MARGIN, 1)

    def rs_copy(step):
        other, device = plane_mate(step)
        return copy(rs_src.at[other], rs_buf.at[plane], rs_ss.at[step], rs_rs.at[step], device)

    def rs_arrival(step):
        other = plane_source(step)
        return copy(rs_src.at[other], rs_buf.at[other], rs_ss.at[step], rs_rs.at[step], up)

    def z_copy(step):
        return copy(z_src, z_buf.at[z], z_ss.at[step], z_rs.at[step], z_mate(step)[1])

    def z_arrival(step):
        other = turn(z + N_Z - step, N_Z)
        return copy(z_src, z_buf.at[other], z_ss.at[step], z_rs.at[step], up)

    def ag_copy(step):
        return copy(ag_buf.at[plane], ag_buf.at[plane], ag_ss.at[step], ag_rs.at[step], plane_mate(step)[1])

    def ag_arrival(step):
        other = plane_source(step)
        return copy(ag_buf.at[other], ag_buf.at[other], ag_ss.at[step], ag_rs.at[step], up)

    def each(count, act):
        for step in range(1, count):
            act(step)

    sent = []

    def go(*copies):
        for one in copies:
            one.start()
            sent.append(one)
        return copies

    def land(copies):
        for one in copies:
            one.wait_recv()

    def both(src, dst, ss, rs, at, first, second):
        return go(
            copy(src(0), dst(0), ss.at[2 * at], rs.at[2 * at], first),
            copy(src(1), dst(1), ss.at[2 * at + 1], rs.at[2 * at + 1], second),
        )

    def tie(upper, lower):
        return pick(half(upper), lower), pick(upper, half(lower))

    if fold:
        pair_copies = go(
            copy(sums.at[pl.ds(2 * (1 - core), 2)], pair_buf.at[pl.ds(0, 2)], pair_ss.at[0], pair_rs.at[0], pair),
            copy(sums.at[pl.ds(4, 1)], pair_buf.at[pl.ds(2, 1)], pair_ss.at[1], pair_rs.at[1], pair),
        )
        fr_copies = {}
        for k in range(2):
            fr_copies[k] = both(
                lambda i: grad.at[k, :, pl.ds(i * (TILE + MARGIN), MARGIN)],
                lambda i: fold_r.at[i, k], fr_ss, fr_rs, k, up, down,
            )
        for k in range(2):
            packs = tie(grad[k, 2, 2 * MARGIN : 3 * MARGIN], grad[k, 2, 3 * MARGIN : 4 * MARGIN])
            for i in range(2):
                mid_s[i, k] = packs[i]
        fm_copies = both(lambda i: mid_s.at[i], lambda i: mid_r.at[i], fm_ss, fm_rs, 0, left, right)

        land(pair_copies)
        for k in range(3):
            own = sums[4] if k == 2 else sums[2 * core + k]
            rs_src[:, k] = own + pair_buf[k]
        each(N_PLANE, lambda s: rs_copy(s).start())
        rs_buf[plane] = rs_src[plane]

        fe_copies = {}

        def fold_rows(k):
            land(fr_copies[k])
            mid[k, :, :MARGIN] = grad[k, :, MARGIN : 2 * MARGIN] + jnp.where(has_up, fold_r[1, k], 0.0)
            mid[k, :, MARGIN:] = grad[k, :, TILE : TILE + MARGIN] + jnp.where(has_down, fold_r[0, k], 0.0)
            packs = tie(mid[k, 2, :MARGIN], mid[k, 2, MARGIN:])
            for i in range(2):
                edge_s[i, k] = packs[i]
            fe_copies[k] = both(
                lambda i: edge_s.at[i, k], lambda i: edge_r.at[i, k], fe_ss, fe_rs, k, left, right
            )

        def block_of(k, block):
            if block in (0, 3):
                start = 0 if block == 0 else MARGIN
                base = [mid[k, part, start : start + MARGIN] for part in range(2)]
                got = edge_r
            else:
                start = MARGIN + block * MARGIN
                base = [grad[k, part, start : start + MARGIN] for part in range(2)]
                got = mid_r
            from_right = jnp.where(has_right, got[0, k], 0.0)
            from_left = jnp.where(has_left, got[1, k], 0.0)
            if block in (0, 1):
                from_right = half(from_right)
            else:
                from_left = half(from_left)
            return base[0] + pick(from_left, 0.0), base[1] + pick(0.0, from_right)

        def update(k, blocks):
            for block in blocks:
                parts = block_of(k, block)
                start = block * MARGIN
                for part in range(2):
                    step = parts[part] * weight_in[part, start : start + MARGIN]
                    cut = slice(part * W, (part + 1) * W)
                    if halo:
                        new = obj_in[k, part, MARGIN + start : 2 * MARGIN + start] - step
                        obj_out[k, part, MARGIN + start : 2 * MARGIN + start] = new
                        tile_out[k, start : start + MARGIN, cut] = new
                    else:
                        obj_out[k, start : start + MARGIN, cut] = step
    else:
        for k in range(2):
            for part in range(2):
                obj_out[k, part, MARGIN : MARGIN + TILE] = obj_in[k, :, part * W : (part + 1) * W]

    hc_copies = {}
    hr_copies = {}
    ho_copies = {}

    def send_cols(k, edge):
        one, two = (MARGIN, TILE) if edge else (2 * MARGIN, 3 * MARGIN)
        at = 2 * k + edge
        first = tie(obj_out[k, 1, one : one + MARGIN], obj_out[k, 1, two : two + MARGIN])[0]
        last = tie(obj_out[k, 0, one : one + MARGIN], obj_out[k, 0, two : two + MARGIN])[1]
        halo_cs[0, at] = last
        halo_cs[1, at] = first
        hc_copies[at] = both(lambda i: halo_cs.at[i, at], lambda i: halo_c.at[i, at], hc_ss, hc_rs, at, left, right)

    def send_rows(k):
        hr_copies[k] = both(
            lambda i: obj_out.at[k, pl.ds(0, 2), pl.ds(MARGIN + i * (TILE - MARGIN), MARGIN)],
            lambda i: halo_r.at[i, k], hr_ss, hr_rs, k, up, down,
        )

    def take_cols(k, edge):
        one, two = (MARGIN, TILE) if edge else (2 * MARGIN, 3 * MARGIN)
        at = 2 * k + edge
        land(hc_copies[at])
        from_right = jnp.where(has_right, halo_c[0, at], 0.0)
        from_left = jnp.where(has_left, halo_c[1, at], 0.0)
        obj_out[k, 2, one : one + MARGIN] = pick(from_right, half(from_left))
        obj_out[k, 2, two : two + MARGIN] = pick(half(from_right), from_left)

    def send_corners(k):
        ho_copies[k] = both(
            lambda i: obj_out.at[k, 2, pl.ds(MARGIN + i * (TILE - MARGIN), MARGIN)],
            lambda i: corner_r.at[i, k], ho_ss, ho_rs, k, up, down,
        )

    if fold:
        fold_rows(0)
        each(N_PLANE, lambda s: rs_arrival(s).wait_recv())
        total = rs_buf[0]
        for other in range(1, N_PLANE):
            total = total + rs_buf[other]
        z_src[...] = total
        z_buf[z] = total
        each(N_Z, lambda s: z_copy(s).start())
        fold_rows(1)
        land(fm_copies)
        for k in range(2):
            update(k, (1, 2))
            if halo:
                send_cols(k, 0)
        for k in range(2):
            land(fe_copies[k])
            update(k, (0, 3))
            if halo:
                send_cols(k, 1)
                send_rows(k)
        each(N_Z, lambda s: z_arrival(s).wait_recv())
        total = z_buf[0]
        for other in range(1, N_Z):
            total = total + z_buf[other]
        probe_weight = 1.0 / (total[2] + PROBE_REG)
        for k in range(2):
            step = total[k] * probe_weight
            ag_buf[plane, k] = probe_in[core, k, plane] - step if halo else step
        each(N_PLANE, lambda s: ag_copy(s).start())
    else:
        own_spots = places_in.at[pl.ds(0, SLOTS)]
        line_copies = both(lambda i: own_spots, lambda i: line_buf.at[2 - 2 * i], spots_ss, spots_rs, 0, left, right)
        for k in range(2):
            send_cols(k, 1)
            send_rows(k)
        for k in range(2):
            send_cols(k, 0)
        line_buf[1] = places_in[:SLOTS]
        land(line_copies)
        spots_copies = both(lambda i: line_buf, lambda i: spots_buf.at[1 - i], spots_ss, spots_rs, 1, up, down)
    if halo:
        for k in range(2):
            take_cols(k, 1)
            send_corners(k)
        for k in range(2):
            take_cols(k, 0)

    if fold:
        each(N_PLANE, lambda s: ag_arrival(s).wait_recv())
        (agp,) = go(copy(ag_buf, ag_pair, agp_ss.at[0], agp_rs.at[0], pair))
        for k in range(2):
            probe_out[core, k] = ag_buf[:, k]

    if halo:
        for k in range(2):
            land(hr_copies[k])
            obj_out[k, :2, TILE + MARGIN :] = jnp.where(has_down, halo_r[0, k], 0.0)
            obj_out[k, :2, :MARGIN] = jnp.where(has_up, halo_r[1, k], 0.0)
        for k in range(2):
            land(ho_copies[k])
            obj_out[k, 2, TILE + MARGIN :] = jnp.where(has_down, corner_r[0, k], 0.0)
            obj_out[k, 2, :MARGIN] = jnp.where(has_up, corner_r[1, k], 0.0)

    if not fold:
        land(spots_copies)

        def packed(spots):
            down_by = spots[:, :1] - (row * TILE - W)
            across = spots[:, 1:2] - (col * TILE - W)
            fits = (down_by > 0) & (down_by < TILE + W) & (across > 0) & (across < TILE + W)
            return jnp.where(fits, down_by * 1024 + across, 0)

        def count_at(far_row, far_col):
            line = places_in[pl.ds(SLOTS + jnp.clip(far_row, 0, N_ROW - 1), 1), :]
            line = jnp.where(lax.broadcasted_iota(jnp.int32, line.shape, 1) == far_col, line, 0)
            inside = jnp.logical_and(far_row >= 0, far_row < N_ROW)
            return jnp.where(inside, jnp.sum(line.astype(jnp.float32), axis=1, keepdims=True), 0.0)

        lists = [spots_buf[0, 0], spots_buf[0, 1], spots_buf[0, 2], line_buf[0], line_buf[2]]
        lists += [spots_buf[1, 0], spots_buf[1, 1], spots_buf[1, 2]]
        own_at = places_in[:SLOTS]
        line_of = lax.broadcasted_iota(jnp.int32, (SLOTS, W), 0)
        lane_of = lax.broadcasted_iota(jnp.int32, (SLOTS, W), 1)
        table = jnp.zeros((SLOTS, W), jnp.int32)
        for i, one in enumerate(lists):
            table = jnp.where(lane_of == i, packed(one), table)
        table = jnp.where(lane_of == ROWS, own_at[:, :1] - (row * TILE - MARGIN), table)
        table = jnp.where(lane_of == COLS, own_at[:, 1:2] - col * TILE, table)
        for i, (below, across) in enumerate(NEAR + ((0, 0),)):
            there = count_at(row + below, col + across).astype(jnp.int32)
            table = jnp.where((lane_of == COUNTS) & (line_of == i), there, table)
        spots_out[...] = table
    if fold:
        land([agp])
        for k in range(2):
            probe_out[1 - core, k] = ag_pair[:, k]
    for one in sent:
        one.wait_send()
    if fold:
        each(N_PLANE, lambda s: rs_copy(s).wait_send())
        each(N_Z, lambda s: z_copy(s).wait_send())
        each(N_PLANE, lambda s: ag_copy(s).wait_send())


def spread(fold, halo, number, *operands):
    vmem = pl.BlockSpec(memory_space=pltpu.VMEM)
    dma = pltpu.SemaphoreType.DMA
    f32 = jnp.float32
    outs = []
    if halo:
        outs.append(jax.ShapeDtypeStruct((2, 3, EXT, W), f32))
    if fold:
        outs.append(jax.ShapeDtypeStruct((2, TILE, TILE), f32))
    else:
        outs.append(jax.ShapeDtypeStruct((SLOTS, W), jnp.int32))
    scratch = []
    if fold:
        outs.append(jax.ShapeDtypeStruct((2, 2, 16, 8, W), f32))
        scratch += [
            pltpu.VMEM((3, 16, 8, W), f32),
            pltpu.VMEM((16, 3, 8, W), f32),
            pltpu.VMEM((16, 3, 8, W), f32),
            pltpu.VMEM((3, 8, W), f32),
            pltpu.VMEM((8, 3, 8, W), f32),
            pltpu.VMEM((16, 2, 8, W), f32),
            pltpu.VMEM((16, 2, 8, W), f32),
            pltpu.VMEM((2, 2, 3, MARGIN, W), f32),
            pltpu.VMEM((2, 3, 2 * MARGIN, W), f32),
            pltpu.VMEM((2, 2, MARGIN, W), f32),
            pltpu.VMEM((2, 2, MARGIN, W), f32),
            pltpu.VMEM((2, 2, MARGIN, W), f32),
            pltpu.VMEM((2, 2, MARGIN, W), f32),
            dma((2,)), dma((2,)), dma((16,)), dma((16,)), dma((8,)), dma((8,)), dma((16,)), dma((16,)),
            dma((1,)), dma((1,)), dma((4,)), dma((4,)), dma((2,)), dma((2,)), dma((4,)), dma((4,)),
        ]
    else:
        scratch += [
            pltpu.VMEM((3, SLOTS, N_COL), jnp.int32),
            pltpu.VMEM((2, 3, SLOTS, N_COL), jnp.int32),
            dma((4,)), dma((4,)),
        ]
    if halo:
        scratch += [
            pltpu.VMEM((2, 4, MARGIN, W), f32),
            pltpu.VMEM((2, 4, MARGIN, W), f32),
            pltpu.VMEM((2, 2, 2, MARGIN, W), f32),
            pltpu.VMEM((2, 2, MARGIN, W), f32),
            dma((8,)), dma((8,)), dma((4,)), dma((4,)), dma((4,)), dma((4,)),
        ]
    return pl.pallas_call(
        functools.partial(spread_kernel, fold, halo),
        out_shape=tuple(outs),
        in_specs=[vmem] * len(operands),
        out_specs=(vmem,) * len(outs),
        scratch_shapes=scratch,
        compiler_params=pltpu.CompilerParams(
            collective_id=number, has_side_effects=True, vmem_limit_bytes=SPREAD_VMEM
        ),
        cost_estimate=pl.CostEstimate(flops=20_000_000_000, bytes_accessed=40_000_000, transcendentals=0),
        name="spread" + str(number),
    )(*operands)


def per_device(object_slab, probe_modes, intensities, positions, live_counts):
    tables = jnp.asarray(dft_parts())
    padded = jnp.pad(positions.reshape(SLOTS, 2), ((0, 0), (0, N_COL - 2)))
    where = jnp.concatenate([padded, live_counts], axis=0)
    intens = intensities.reshape(SLOTS, W, W)
    probe = probe_modes
    current, spots = spread(False, True, 0, object_slab, where)
    for sweep in range(ITERS):
        grad, sums, weight = frames(spots, current, probe, intens, tables)
        last = sweep == ITERS - 1
        outs = spread(
            True, not last, sweep + 1,
            current, probe.reshape(2, 2, 16, 8, W), grad, sums.reshape(5, 16, 8, W), weight,
        )
        if last:
            return tile - outs[0], probe - outs[1].reshape(2, 2, W, W)
        current, tile, probe = outs
        probe = probe.reshape(2, 2, W, W)


def solution(mesh):
    return jax.shard_map(
        per_device,
        mesh=mesh,
        in_specs=(
            P(None, "row", "col"),
            P(),
            P("row", "col", None, None, None),
            P("row", "col", None, None),
            P(),
        ),
        out_specs=(P(None, "row", "col"), P()),
        check_vma=False,
    )
```

```python
import functools

import jax
import jax.numpy as jnp
import ml_dtypes
import numpy as np
from jax import lax
from jax.experimental import pallas as pl
from jax.experimental.pallas import tpu as pltpu
from jax.sharding import PartitionSpec as P

ITERS = 2
W = 128
MARGIN = 64
TILE = 256
EXT = TILE + 2 * MARGIN
SLOTS = 24
BATCH = 1
RING = 8
GAP = 2
UNROLL = 3
ORDER = 321546
OBJECT_REG = 1.0
PROBE_REG = 1.0
FLOOR_SQ = 0.0625
TINY = 1e-36
N_ROW = 32
N_COL = 8
N_PLANE = 16
N_Z = 8
FRAMES_VMEM = 20 * 1024 * 1024
SPREAD_VMEM = 16 * 1024 * 1024
MESH = pl.DeviceIdType.MESH
NEAR = ((-1, -1), (-1, 0), (-1, 1), (0, -1), (0, 1), (1, -1), (1, 0), (1, 1))
CHUNK = 8
ROWS, COLS, COUNTS = 8, 9, 10


def dft_parts():
    counter = np.arange(W)
    angles = (counter[:, None] * counter[None, :] % W) * (2.0 * np.pi / W)
    cosine = np.cos(angles) / np.sqrt(W)
    sine = np.sin(angles) / np.sqrt(W)
    fore = np.block([[cosine, sine], [-sine, cosine]])
    back = np.block([[cosine, -sine], [sine, cosine]])

    def split(table):
        high = table.astype(np.float32).astype(ml_dtypes.bfloat16)
        low = (table - high.astype(np.float64)).astype(np.float32).astype(ml_dtypes.bfloat16)
        return high, low

    fore_hi, fore_lo = split(fore)
    back_hi, back_lo = split(back)
    return np.stack([fore_hi, fore_lo, back_hi, back_lo])


def split_two(value):
    high = value.astype(jnp.bfloat16)
    low = (value - high.astype(jnp.float32)).astype(jnp.bfloat16)
    return high, low


def dot(left, right):
    return jnp.dot(left, right, preferred_element_type=jnp.float32)


def frames_kernel(
    spots, obj, probe_in, intens, tables_in,
    grad, sums, weight, patch_buf, mid_buf, far_buf, back_buf, near_buf, light_buf, illum, listed, tables, gap, probe,
):
    probe[...] = probe_in[...]
    tables[...] = tables_in[...]
    grad[...] = jnp.zeros_like(grad)
    sums[...] = jnp.zeros_like(sums)
    lighting = probe[0, 0] * probe[0, 0] + probe[0, 1] * probe[0, 1]
    light_buf[...] = lighting + probe[1, 0] * probe[1, 0] + probe[1, 1] * probe[1, 1]
    own = spots[len(NEAR), COUNTS]

    def on_left(high):
        return jnp.concatenate([tables[high], tables[high + 1], tables[high]], axis=1)

    def on_right(high):
        return jnp.concatenate([tables[high], tables[high], tables[high + 1]], axis=0)

    lane = lax.broadcasted_iota(jnp.int32, (W, W), 1)

    def place(slot):
        row = spots[slot, ROWS]
        col = spots[slot, COLS]
        col = jnp.where(col < 0, col + EXT, col)
        first = lax.shift_right_logical(col, 7)
        shift = lax.bitwise_and(col, 127)
        second = jnp.where(first == 2, 0, first + 1)
        return row, first, second, shift

    def member_slot(turn, member):
        slot = turn * BATCH + member
        flag = jnp.where(jnp.logical_and(slot >= 0, slot < own), 1.0, 0.0).astype(jnp.float32)
        return jnp.clip(slot, 0, SLOTS - 1), flag

    def last_product(turn):
        halves = []
        for member in range(BATCH):
            for m in range(2):
                halves.append(jnp.concatenate([near_buf[member, m], near_buf[member, m, :, : 2 * W]], axis=1))
        return dot(jnp.concatenate(halves, axis=0), on_right(0))

    def last_adds(turn, resid):
        ring = lax.bitwise_and(turn, RING - 1)
        terms = [None] * 5
        for member in range(BATCH):
            slot, flag = member_slot(turn, member)
            row, first, second, shift = place(slot)
            keep = lane >= shift
            obj_real = patch_buf[ring, member, 0]
            obj_imag = patch_buf[ring, member, 1]
            grad_real = 0.0
            grad_imag = 0.0
            adds = []
            for m in range(2):
                base = (member * 2 + m) * W
                real = resid[base : base + W, :W]
                imag = resid[base : base + W, W:]
                grad_real = grad_real + probe[m, 0] * real + probe[m, 1] * imag
                grad_imag = grad_imag + probe[m, 0] * imag - probe[m, 1] * real
                adds.append(obj_real * real + obj_imag * imag)
                adds.append(obj_real * imag - obj_imag * real)
            adds.append((obj_real * obj_real + obj_imag * obj_imag) * flag)
            for k in range(5):
                terms[k] = adds[k] if member == 0 else terms[k] + adds[k]
            for k, piece in enumerate((grad_real, grad_imag)):
                turned = pltpu.roll(piece, shift, 1)
                grad[k, first, pl.ds(row, W), :] += jnp.where(keep, turned, 0.0)
                grad[k, second, pl.ds(row, W), :] += jnp.where(keep, 0.0, turned)
            turned = pltpu.roll(light_buf[...] * flag, shift, 1)
            at = jnp.where(first == 2, 0, first + 1)
            illum[at, pl.ds(row + MARGIN, W), :] += jnp.where(keep, turned, 0.0)
            illum[at + 1, pl.ds(row + MARGIN, W), :] += jnp.where(keep, 0.0, turned)
        for k in range(5):
            sums[k] += terms[k]

    def third_stage(turn):
        for member in range(BATCH):
            stacked = jnp.concatenate([back_buf[member, :256], back_buf[member]], axis=0)
            near = dot(on_left(2), stacked)
            real_hi, real_lo = split_two(near[:W])
            imag_hi, imag_lo = split_two(near[W:])
            for m in range(2):
                cut = slice(m * W, (m + 1) * W)
                near_buf[member, m] = jnp.concatenate(
                    [real_hi[:, cut], imag_hi[:, cut], real_lo[:, cut], imag_lo[:, cut]], axis=1
                )

    def scale(turn, far=None):
        for member in range(BATCH):
            slot, flag = member_slot(turn, member)
            far_real = far_buf[member, :W] if far is None else far[member][:W]
            far_imag = far_buf[member, W:] if far is None else far[member][W:]
            power = far_real * far_real + far_imag * far_imag
            model = jnp.maximum(power[:, :W] + power[:, W:], FLOOR_SQ)
            frame = intens[slot]
            ratio = frame * lax.rsqrt(jnp.maximum(frame * model, TINY))
            factor = (1.0 - ratio) * flag
            factor = jnp.concatenate([factor, factor], axis=1)
            real_hi, real_lo = split_two(far_real * factor)
            imag_hi, imag_lo = split_two(far_imag * factor)
            back_buf[member] = jnp.concatenate([real_hi, imag_hi, real_lo, imag_lo], axis=0)

    def second_stage(turn):
        for member in range(BATCH):
            stacked = jnp.concatenate([mid_buf[member, :256], mid_buf[member]], axis=0)
            far_buf[member] = dot(on_left(0), stacked)

    def first_stage(turn):
        ring = lax.bitwise_and(turn, RING - 1)
        rows = []
        for member in range(BATCH):
            slot, flag = member_slot(turn, member)
            row, first, second, shift = place(slot)
            back = lax.bitwise_and(128 - shift, 127)
            keep = lane >= shift
            patch = []
            for k in range(2):
                one = obj[k, first, pl.ds(row, W), :]
                two = obj[k, second, pl.ds(row, W), :]
                patch.append(pltpu.roll(jnp.where(keep, one, two), back, 1))
                patch_buf[ring, member, k] = patch[k]
            for m in range(2):
                real_hi, real_lo = split_two(probe[m, 0] * patch[0] - probe[m, 1] * patch[1])
                imag_hi, imag_lo = split_two(probe[m, 0] * patch[1] + probe[m, 1] * patch[0])
                rows.append(
                    jnp.concatenate([real_hi, imag_hi, real_lo, imag_lo, real_hi, imag_hi], axis=1)
                )
        mid = dot(jnp.concatenate(rows, axis=0), on_right(2))
        for member in range(BATCH):
            base = member * 2 * W
            real_hi, real_lo = split_two(
                jnp.concatenate([mid[base : base + W, :W], mid[base + W : base + 2 * W, :W]], axis=1)
            )
            imag_hi, imag_lo = split_two(
                jnp.concatenate([mid[base : base + W, W:], mid[base + W : base + 2 * W, W:]], axis=1)
            )
            mid_buf[member] = jnp.concatenate([real_hi, imag_hi, real_lo, imag_lo], axis=0)

    illum[...] = jnp.zeros_like(illum)
    held_count = jnp.int32(0)
    for near in range(len(NEAR)):
        there = spots[near, COUNTS]

        def gather(chunk, held):
            for k in range(CHUNK):
                slot = chunk * CHUNK + k
                packed = spots[slot, near]
                listed[held] = packed
                fits = jnp.logical_and(packed > 0, slot < there)
                held = held + jnp.where(fits, 1, 0)
            return held

        held_count = lax.fori_loop(0, (there + CHUNK - 1) // CHUNK, gather, held_count)

    def shine(step, carry):
        for k in range(2):
            entry = 2 * step + k
            live = entry < held_count
            packed = jnp.where(live, listed[jnp.where(live, entry, 0)], 1025)
            flag = jnp.where(live, 1.0, 0.0).astype(jnp.float32)
            row = lax.shift_right_logical(packed, 10)
            col = lax.bitwise_and(packed, 1023)
            first = lax.shift_right_logical(col, 7)
            shift = lax.bitwise_and(col, 127)
            keep = lane >= shift
            turned = pltpu.roll(light_buf[...] * flag, shift, 1)
            illum[first, pl.ds(row, W), :] += jnp.where(keep, turned, 0.0)
            illum[first + 1, pl.ds(row, W), :] += jnp.where(keep, 0.0, turned)
        return carry

    lax.fori_loop(0, (held_count + 1) // 2, shine, 0)

    order = str(ORDER)
    lag = {}
    for before, now in zip(" 12345", "123456"):
        lag[now] = 0 if before == " " else lag[before] + (order.index(now) < order.index(before))

    def body(turn, runs):
        held = None
        for stage in order:
            if not runs(lag[stage]):
                continue
            at = turn - lag[stage]
            if stage == "1":
                first_stage(at)
            elif stage == "2":
                second_stage(at)
            elif stage == "3":
                scale(at)
            elif stage == "4":
                third_stage(at)
            elif stage == "5":
                held = last_product(at)
            else:
                last_adds(at, held)

    depth = lag["6"]
    rounds = (jnp.maximum(own - depth, 0) + UNROLL - 1) // UNROLL

    def several(step, carry):
        for k in range(UNROLL):
            body(step * UNROLL + depth + k, lambda late: True)
        return carry

    for k in range(depth):
        body(jnp.int32(k), lambda late: late <= k)
    lax.fori_loop(0, rounds, several, 0)
    for k in range(depth):
        body(rounds * UNROLL + depth + k, lambda late: late > k)
    for part in range(2):
        weight[part] = 1.0 / (illum[part + 1, W : W + TILE, :] + OBJECT_REG)


def frames(spots, obj, probe, intens, tables):
    vmem = pl.BlockSpec(memory_space=pltpu.VMEM)
    smem = pl.BlockSpec(memory_space=pltpu.SMEM)
    return pl.pallas_call(
        frames_kernel,
        out_shape=(
            jax.ShapeDtypeStruct((2, 3, EXT, W), jnp.float32),
            jax.ShapeDtypeStruct((5, W, W), jnp.float32),
            jax.ShapeDtypeStruct((2, TILE, W), jnp.float32),
        ),
        in_specs=[smem] + [vmem] * 4,
        out_specs=(vmem, vmem, vmem),
        scratch_shapes=[
            pltpu.VMEM((RING, BATCH, 2, W, W), jnp.float32),
            pltpu.VMEM((BATCH, 4 * W, 2 * W), jnp.bfloat16),
            pltpu.VMEM((BATCH, 2 * W, 2 * W), jnp.float32),
            pltpu.VMEM((BATCH, 4 * W, 2 * W), jnp.bfloat16),
            pltpu.VMEM((BATCH, 2, W, 4 * W), jnp.bfloat16),
            pltpu.VMEM((W, W), jnp.float32),
            pltpu.VMEM((4, 2 * TILE, W), jnp.float32),
            pltpu.SMEM((len(NEAR) * SLOTS + CHUNK,), jnp.int32),
            pltpu.VMEM((4, 2 * W, 2 * W), jnp.bfloat16),
            pltpu.VMEM((GAP * 8, W), jnp.float32),
            pltpu.VMEM((2, 2, W, W), jnp.float32),
        ],
        compiler_params=pltpu.CompilerParams(vmem_limit_bytes=FRAMES_VMEM),
        cost_estimate=pl.CostEstimate(flops=9_600_000_000, bytes_accessed=10_000_000, transcendentals=0),
        name="frames",
    )(spots, obj, probe, intens, tables)


def own_place():
    row = lax.axis_index("row")
    col = lax.axis_index("col")
    core = row % 2
    z_hi = (row // 2) % 4
    x = row // 8
    y = col // 2
    z_lo = col % 2
    return row, col, core, x, y, z_hi, z_lo


def spread_kernel(fold, halo, *refs):
    refs = list(refs)
    take = lambda n: [refs.pop(0) for _ in range(n)]
    if fold:
        obj_in, probe_in, grad, sums, weight_in = take(5)
    else:
        obj_in, places_in = take(2)
    (obj_out,) = take(1)
    if not fold:
        (spots_out,) = take(1)
        line_buf, spots_buf, spots_ss, spots_rs = take(4)
    if fold:
        if halo:
            (tile_out,) = take(1)
        (probe_out,) = take(1)
        (pair_buf, rs_src, rs_buf, z_src, z_buf, ag_buf, ag_pair, fold_r, mid, mid_s, mid_r, edge_s, edge_r) = take(13)
        (pair_ss, pair_rs, rs_ss, rs_rs, z_ss, z_rs, ag_ss, ag_rs, agp_ss, agp_rs) = take(10)
        (fr_ss, fr_rs, fm_ss, fm_rs, fe_ss, fe_rs) = take(6)
    if halo:
        halo_cs, halo_c, halo_r, corner_r, hc_ss, hc_rs, hr_ss, hr_rs, ho_ss, ho_rs = take(10)

    row, col, core, x, y, z_hi, z_lo = own_place()
    plane = x * 4 + y
    z = z_hi * 2 + z_lo
    up = (lax.rem(row + N_ROW - 1, N_ROW), col)
    down = (lax.rem(row + 1, N_ROW), col)
    left = (row, lax.rem(col + N_COL - 1, N_COL))
    right = (row, lax.rem(col + 1, N_COL))
    pair = (row + 1 - 2 * core, col)
    has_up = row > 0
    has_down = row < N_ROW - 1
    has_left = col > 0
    has_right = col < N_COL - 1

    def turn(value, size):
        return jnp.where(value >= size, value - size, value)

    def plane_mate(step):
        far_x = turn(x + step // 4, 4)
        far_y = turn(y + step % 4, 4)
        return far_x * 4 + far_y, ((far_x * 4 + z_hi) * 2 + core, far_y * 2 + z_lo)

    def plane_source(step):
        return turn(x + (4 - step // 4) % 4, 4) * 4 + turn(y + (4 - step % 4) % 4, 4)

    def z_mate(step):
        other = turn(z + step, N_Z)
        return other, ((x * 4 + other // 2) * 2 + core, y * 2 + other % 2)

    def copy(src, dst, ss, rs, device):
        return pltpu.make_async_remote_copy(
            src_ref=src, dst_ref=dst, send_sem=ss, recv_sem=rs, device_id=device, device_id_type=MESH
        )

    barrier = pltpu.get_barrier_semaphore()

    def greet(device):
        pl.semaphore_signal(barrier, inc=1, device_id=device, device_id_type=MESH)

    for device in (up, down, left, right):
        greet(device)
    greeted = 4
    if fold:
        greet(pair)
        for step in range(1, N_PLANE):
            greet(plane_mate(step)[1])
        for step in range(1, N_Z):
            greet(z_mate(step)[1])
        greeted += 1 + N_PLANE - 1 + N_Z - 1
    pl.semaphore_wait(barrier, greeted)

    def pick(first, second):
        shape = jnp.shape(first) or jnp.shape(second)
        return jnp.where(lax.broadcasted_iota(jnp.int32, shape, 1) < MARGIN, first, second)

    def half(value):
        return pltpu.roll(value, MARGIN, 1)

    def rs_copy(step):
        other, device = plane_mate(step)
        return copy(rs_src.at[other], rs_buf.at[plane], rs_ss.at[step], rs_rs.at[step], device)

    def rs_arrival(step):
        other = plane_source(step)
        return copy(rs_src.at[other], rs_buf.at[other], rs_ss.at[step], rs_rs.at[step], up)

    def z_copy(step):
        return copy(z_src, z_buf.at[z], z_ss.at[step], z_rs.at[step], z_mate(step)[1])

    def z_arrival(step):
        other = turn(z + N_Z - step, N_Z)
        return copy(z_src, z_buf.at[other], z_ss.at[step], z_rs.at[step], up)

    def ag_copy(step):
        return copy(ag_buf.at[plane], ag_buf.at[plane], ag_ss.at[step], ag_rs.at[step], plane_mate(step)[1])

    def ag_arrival(step):
        other = plane_source(step)
        return copy(ag_buf.at[other], ag_buf.at[other], ag_ss.at[step], ag_rs.at[step], up)

    def each(count, act):
        for step in range(1, count):
            act(step)

    sent = []

    def go(*copies):
        for one in copies:
            one.start()
            sent.append(one)
        return copies

    def land(copies):
        for one in copies:
            one.wait_recv()

    def both(src, dst, ss, rs, at, first, second):
        return go(
            copy(src(0), dst(0), ss.at[2 * at], rs.at[2 * at], first),
            copy(src(1), dst(1), ss.at[2 * at + 1], rs.at[2 * at + 1], second),
        )

    def tie(upper, lower):
        return pick(half(upper), lower), pick(upper, half(lower))

    if fold:
        pair_copies = go(
            copy(sums.at[pl.ds(2 * (1 - core), 2)], pair_buf.at[pl.ds(0, 2)], pair_ss.at[0], pair_rs.at[0], pair),
            copy(sums.at[pl.ds(4, 1)], pair_buf.at[pl.ds(2, 1)], pair_ss.at[1], pair_rs.at[1], pair),
        )
        fr_copies = {}
        for k in range(2):
            fr_copies[k] = both(
                lambda i: grad.at[k, :, pl.ds(i * (TILE + MARGIN), MARGIN)],
                lambda i: fold_r.at[i, k], fr_ss, fr_rs, k, up, down,
            )
        for k in range(2):
            packs = tie(grad[k, 2, 2 * MARGIN : 3 * MARGIN], grad[k, 2, 3 * MARGIN : 4 * MARGIN])
            for i in range(2):
                mid_s[i, k] = packs[i]
        fm_copies = both(lambda i: mid_s.at[i], lambda i: mid_r.at[i], fm_ss, fm_rs, 0, left, right)

        land(pair_copies)
        for k in range(3):
            own = sums[4] if k == 2 else sums[2 * core + k]
            rs_src[:, k] = own + pair_buf[k]
        each(N_PLANE, lambda s: rs_copy(s).start())
        rs_buf[plane] = rs_src[plane]

        fe_copies = {}

        def fold_rows(k):
            land(fr_copies[k])
            mid[k, :, :MARGIN] = grad[k, :, MARGIN : 2 * MARGIN] + jnp.where(has_up, fold_r[1, k], 0.0)
            mid[k, :, MARGIN:] = grad[k, :, TILE : TILE + MARGIN] + jnp.where(has_down, fold_r[0, k], 0.0)
            packs = tie(mid[k, 2, :MARGIN], mid[k, 2, MARGIN:])
            for i in range(2):
                edge_s[i, k] = packs[i]
            fe_copies[k] = both(
                lambda i: edge_s.at[i, k], lambda i: edge_r.at[i, k], fe_ss, fe_rs, k, left, right
            )

        def block_of(k, block):
            if block in (0, 3):
                start = 0 if block == 0 else MARGIN
                base = [mid[k, part, start : start + MARGIN] for part in range(2)]
                got = edge_r
            else:
                start = MARGIN + block * MARGIN
                base = [grad[k, part, start : start + MARGIN] for part in range(2)]
                got = mid_r
            from_right = jnp.where(has_right, got[0, k], 0.0)
            from_left = jnp.where(has_left, got[1, k], 0.0)
            if block in (0, 1):
                from_right = half(from_right)
            else:
                from_left = half(from_left)
            return base[0] + pick(from_left, 0.0), base[1] + pick(0.0, from_right)

        def update(k, blocks):
            for block in blocks:
                parts = block_of(k, block)
                start = block * MARGIN
                for part in range(2):
                    step = parts[part] * weight_in[part, start : start + MARGIN]
                    cut = slice(part * W, (part + 1) * W)
                    if halo:
                        new = obj_in[k, part, MARGIN + start : 2 * MARGIN + start] - step
                        obj_out[k, part, MARGIN + start : 2 * MARGIN + start] = new
                        tile_out[k, start : start + MARGIN, cut] = new
                    else:
                        obj_out[k, start : start + MARGIN, cut] = step
    else:
        for k in range(2):
            for part in range(2):
                obj_out[k, part, MARGIN : MARGIN + TILE] = obj_in[k, :, part * W : (part + 1) * W]

    hc_copies = {}
    hr_copies = {}
    ho_copies = {}

    def send_cols(k, edge):
        one, two = (MARGIN, TILE) if edge else (2 * MARGIN, 3 * MARGIN)
        at = 2 * k + edge
        first = tie(obj_out[k, 1, one : one + MARGIN], obj_out[k, 1, two : two + MARGIN])[0]
        last = tie(obj_out[k, 0, one : one + MARGIN], obj_out[k, 0, two : two + MARGIN])[1]
        halo_cs[0, at] = last
        halo_cs[1, at] = first
        hc_copies[at] = both(lambda i: halo_cs.at[i, at], lambda i: halo_c.at[i, at], hc_ss, hc_rs, at, left, right)

    def send_rows(k):
        hr_copies[k] = both(
            lambda i: obj_out.at[k, pl.ds(0, 2), pl.ds(MARGIN + i * (TILE - MARGIN), MARGIN)],
            lambda i: halo_r.at[i, k], hr_ss, hr_rs, k, up, down,
        )

    def take_cols(k, edge):
        one, two = (MARGIN, TILE) if edge else (2 * MARGIN, 3 * MARGIN)
        at = 2 * k + edge
        land(hc_copies[at])
        from_right = jnp.where(has_right, halo_c[0, at], 0.0)
        from_left = jnp.where(has_left, halo_c[1, at], 0.0)
        obj_out[k, 2, one : one + MARGIN] = pick(from_right, half(from_left))
        obj_out[k, 2, two : two + MARGIN] = pick(half(from_right), from_left)

    def send_corners(k):
        ho_copies[k] = both(
            lambda i: obj_out.at[k, 2, pl.ds(MARGIN + i * (TILE - MARGIN), MARGIN)],
            lambda i: corner_r.at[i, k], ho_ss, ho_rs, k, up, down,
        )

    if fold:
        fold_rows(0)
        each(N_PLANE, lambda s: rs_arrival(s).wait_recv())
        total = rs_buf[0]
        for other in range(1, N_PLANE):
            total = total + rs_buf[other]
        z_src[...] = total
        z_buf[z] = total
        each(N_Z, lambda s: z_copy(s).start())
        fold_rows(1)
        land(fm_copies)
        for k in range(2):
            update(k, (1, 2))
            if halo:
                send_cols(k, 0)
        for k in range(2):
            land(fe_copies[k])
            update(k, (0, 3))
            if halo:
                send_cols(k, 1)
                send_rows(k)
        each(N_Z, lambda s: z_arrival(s).wait_recv())
        total = z_buf[0]
        for other in range(1, N_Z):
            total = total + z_buf[other]
        probe_weight = 1.0 / (total[2] + PROBE_REG)
        for k in range(2):
            step = total[k] * probe_weight
            ag_buf[plane, k] = probe_in[core, k, plane] - step if halo else step
        each(N_PLANE, lambda s: ag_copy(s).start())
    else:
        own_spots = places_in.at[pl.ds(0, SLOTS)]
        line_copies = both(lambda i: own_spots, lambda i: line_buf.at[2 - 2 * i], spots_ss, spots_rs, 0, left, right)
        for k in range(2):
            send_cols(k, 1)
            send_rows(k)
        for k in range(2):
            send_cols(k, 0)
        line_buf[1] = places_in[:SLOTS]
        land(line_copies)
        spots_copies = both(lambda i: line_buf, lambda i: spots_buf.at[1 - i], spots_ss, spots_rs, 1, up, down)
    if halo:
        for k in range(2):
            take_cols(k, 1)
            send_corners(k)
        for k in range(2):
            take_cols(k, 0)

    if fold:
        each(N_PLANE, lambda s: ag_arrival(s).wait_recv())
        (agp,) = go(copy(ag_buf, ag_pair, agp_ss.at[0], agp_rs.at[0], pair))
        for k in range(2):
            probe_out[core, k] = ag_buf[:, k]

    if halo:
        for k in range(2):
            land(hr_copies[k])
            obj_out[k, :2, TILE + MARGIN :] = jnp.where(has_down, halo_r[0, k], 0.0)
            obj_out[k, :2, :MARGIN] = jnp.where(has_up, halo_r[1, k], 0.0)
        for k in range(2):
            land(ho_copies[k])
            obj_out[k, 2, TILE + MARGIN :] = jnp.where(has_down, corner_r[0, k], 0.0)
            obj_out[k, 2, :MARGIN] = jnp.where(has_up, corner_r[1, k], 0.0)

    if not fold:
        land(spots_copies)

        def packed(spots):
            down_by = spots[:, :1] - (row * TILE - W)
            across = spots[:, 1:2] - (col * TILE - W)
            fits = (down_by > 0) & (down_by < TILE + W) & (across > 0) & (across < TILE + W)
            return jnp.where(fits, down_by * 1024 + across, 0)

        def count_at(far_row, far_col):
            line = places_in[pl.ds(SLOTS + jnp.clip(far_row, 0, N_ROW - 1), 1), :]
            line = jnp.where(lax.broadcasted_iota(jnp.int32, line.shape, 1) == far_col, line, 0)
            inside = jnp.logical_and(far_row >= 0, far_row < N_ROW)
            return jnp.where(inside, jnp.sum(line.astype(jnp.float32), axis=1, keepdims=True), 0.0)

        lists = [spots_buf[0, 0], spots_buf[0, 1], spots_buf[0, 2], line_buf[0], line_buf[2]]
        lists += [spots_buf[1, 0], spots_buf[1, 1], spots_buf[1, 2]]
        own_at = places_in[:SLOTS]
        line_of = lax.broadcasted_iota(jnp.int32, (SLOTS, W), 0)
        lane_of = lax.broadcasted_iota(jnp.int32, (SLOTS, W), 1)
        table = jnp.zeros((SLOTS, W), jnp.int32)
        for i, one in enumerate(lists):
            table = jnp.where(lane_of == i, packed(one), table)
        table = jnp.where(lane_of == ROWS, own_at[:, :1] - (row * TILE - MARGIN), table)
        table = jnp.where(lane_of == COLS, own_at[:, 1:2] - col * TILE, table)
        for i, (below, across) in enumerate(NEAR + ((0, 0),)):
            there = count_at(row + below, col + across).astype(jnp.int32)
            table = jnp.where((lane_of == COUNTS) & (line_of == i), there, table)
        spots_out[...] = table
    if fold:
        land([agp])
        for k in range(2):
            probe_out[1 - core, k] = ag_pair[:, k]
    for one in sent:
        one.wait_send()
    if fold:
        each(N_PLANE, lambda s: rs_copy(s).wait_send())
        each(N_Z, lambda s: z_copy(s).wait_send())
        each(N_PLANE, lambda s: ag_copy(s).wait_send())


def spread(fold, halo, number, *operands):
    vmem = pl.BlockSpec(memory_space=pltpu.VMEM)
    dma = pltpu.SemaphoreType.DMA
    f32 = jnp.float32
    outs = []
    if halo:
        outs.append(jax.ShapeDtypeStruct((2, 3, EXT, W), f32))
    if fold:
        outs.append(jax.ShapeDtypeStruct((2, TILE, TILE), f32))
    else:
        outs.append(jax.ShapeDtypeStruct((SLOTS, W), jnp.int32))
    scratch = []
    if fold:
        outs.append(jax.ShapeDtypeStruct((2, 2, 16, 8, W), f32))
        scratch += [
            pltpu.VMEM((3, 16, 8, W), f32),
            pltpu.VMEM((16, 3, 8, W), f32),
            pltpu.VMEM((16, 3, 8, W), f32),
            pltpu.VMEM((3, 8, W), f32),
            pltpu.VMEM((8, 3, 8, W), f32),
            pltpu.VMEM((16, 2, 8, W), f32),
            pltpu.VMEM((16, 2, 8, W), f32),
            pltpu.VMEM((2, 2, 3, MARGIN, W), f32),
            pltpu.VMEM((2, 3, 2 * MARGIN, W), f32),
            pltpu.VMEM((2, 2, MARGIN, W), f32),
            pltpu.VMEM((2, 2, MARGIN, W), f32),
            pltpu.VMEM((2, 2, MARGIN, W), f32),
            pltpu.VMEM((2, 2, MARGIN, W), f32),
            dma((2,)), dma((2,)), dma((16,)), dma((16,)), dma((8,)), dma((8,)), dma((16,)), dma((16,)),
            dma((1,)), dma((1,)), dma((4,)), dma((4,)), dma((2,)), dma((2,)), dma((4,)), dma((4,)),
        ]
    else:
        scratch += [
            pltpu.VMEM((3, SLOTS, N_COL), jnp.int32),
            pltpu.VMEM((2, 3, SLOTS, N_COL), jnp.int32),
            dma((4,)), dma((4,)),
        ]
    if halo:
        scratch += [
            pltpu.VMEM((2, 4, MARGIN, W), f32),
            pltpu.VMEM((2, 4, MARGIN, W), f32),
            pltpu.VMEM((2, 2, 2, MARGIN, W), f32),
            pltpu.VMEM((2, 2, MARGIN, W), f32),
            dma((8,)), dma((8,)), dma((4,)), dma((4,)), dma((4,)), dma((4,)),
        ]
    return pl.pallas_call(
        functools.partial(spread_kernel, fold, halo),
        out_shape=tuple(outs),
        in_specs=[vmem] * len(operands),
        out_specs=(vmem,) * len(outs),
        scratch_shapes=scratch,
        compiler_params=pltpu.CompilerParams(
            collective_id=number, has_side_effects=True, vmem_limit_bytes=SPREAD_VMEM
        ),
        cost_estimate=pl.CostEstimate(flops=20_000_000_000, bytes_accessed=40_000_000, transcendentals=0),
        name="spread" + str(number),
    )(*operands)


def per_device(object_slab, probe_modes, intensities, positions, live_counts):
    tables = jnp.asarray(dft_parts())
    padded = jnp.pad(positions.reshape(SLOTS, 2), ((0, 0), (0, N_COL - 2)))
    where = jnp.concatenate([padded, live_counts], axis=0)
    intens = intensities.reshape(SLOTS, W, W)
    probe = probe_modes
    current, spots = spread(False, True, 0, object_slab, where)
    for sweep in range(ITERS):
        grad, sums, weight = frames(spots, current, probe, intens, tables)
        last = sweep == ITERS - 1
        outs = spread(
            True, not last, sweep + 1,
            current, probe.reshape(2, 2, 16, 8, W), grad, sums.reshape(5, 16, 8, W), weight,
        )
        if last:
            return tile - outs[0], probe - outs[1].reshape(2, 2, W, W)
        current, tile, probe = outs
        probe = probe.reshape(2, 2, W, W)


def solution(mesh):
    return jax.shard_map(
        per_device,
        mesh=mesh,
        in_specs=(
            P(None, "row", "col"),
            P(),
            P("row", "col", None, None, None),
            P("row", "col", None, None),
            P(),
        ),
        out_specs=(P(None, "row", "col"), P()),
        check_vma=False,
    )
```
